128 devices in a mesh: pipe: 2 (over z_lo), dp: 64 (over x, z_hi, y, core).
Axes of the slice: x: 4, y: 4, z: 4 (z_hi: 2, z_lo: 2; z = z_hi * 2 + z_lo), core: 2. Of those that a mesh axis runs over, the one named last changes fastest.
Arguments:
- pixels: float32 [128, 588, 1536], P('dp', None, 'pipe')
- visible_counts: int32 [128], P('dp'), may hold values from 58 to 235, as said below
- visible_index: int32 [128, 235], P('dp'), may hold values from 0 to 587, as said below
- running_mean: float32 [6], P('pipe'), may hold values from -1 to 1
- running_var: float32 [6], P('pipe'), may hold values from 0.5 to 2
- patch_weight: bfloat16 [1536, 768], P(('pipe', 'dp')), may hold values from -0.15625 to 0.15625
- patch_bias: bfloat16 [768], P(('pipe', 'dp')), may hold values from -1.75 to 1.75
- enc_ln1_gain: bfloat16 [768], P(('pipe', 'dp')), may hold values from 0.5 to 1.5
- enc_ln1_shift: bfloat16 [768], P(('pipe', 'dp')), may hold values from -1.25 to 1.25
- enc_qkv_weight: bfloat16 [768, 2304], P(('pipe', 'dp')), may hold values from -0.21875 to 0.21875
- enc_qv_bias: bfloat16 [1536], P(('pipe', 'dp')), may hold values from -1.25 to 1.25
- enc_out_weight: bfloat16 [768, 768], P(('pipe', 'dp')), may hold values from -0.875 to 0.875
- enc_out_bias: bfloat16 [768], P(('pipe', 'dp')), may hold values from -1.25 to 1.25
- enc_ln2_gain: bfloat16 [768], P(('pipe', 'dp')), may hold values from 0.5 to 1.5
- enc_ln2_shift: bfloat16 [768], P(('pipe', 'dp')), may hold values from -1.25 to 1.25
- enc_up_weight: bfloat16 [768, 3072], P(('pipe', 'dp')), may hold values from -0.21875 to 0.21875
- enc_up_bias: bfloat16 [3072], P(('pipe', 'dp')), may hold values from -1.25 to 1.25
- enc_down_weight: bfloat16 [3072, 768], P(('pipe', 'dp')), may hold values from -0.109375 to 0.109375
- enc_down_bias: bfloat16 [768], P(('pipe', 'dp')), may hold values from -1.25 to 1.25
- dec_embed_weight: bfloat16 [768, 512], P(('pipe', 'dp')), may hold values from -0.21875 to 0.21875
- dec_embed_bias: bfloat16 [512], P(('pipe', 'dp')), may hold values from -1.75 to 1.75
- mask_token: bfloat16 [512], P(('pipe', 'dp')), may hold values from -6 to 6
- dec_ln1_gain: bfloat16 [512], P(('pipe', 'dp')), may hold values from 0.5 to 1.5
- dec_ln1_shift: bfloat16 [512], P(('pipe', 'dp')), may hold values from -1.25 to 1.25
- dec_qkv_weight: bfloat16 [512, 1536], P(('pipe', 'dp')), may hold values from -0.25 to 0.25
- dec_qv_bias: bfloat16 [1024], P(('pipe', 'dp')), may hold values from -1.25 to 1.25
- dec_out_weight: bfloat16 [512, 512], P(('pipe', 'dp')), may hold values from -1 to 1
- dec_out_bias: bfloat16 [512], P(('pipe', 'dp')), may hold values from -1.25 to 1.25
- dec_ln2_gain: bfloat16 [512], P(('pipe', 'dp')), may hold values from 0.5 to 1.5
- dec_ln2_shift: bfloat16 [512], P(('pipe', 'dp')), may hold values from -1.25 to 1.25
- dec_up_weight: bfloat16 [512, 2048], P(('pipe', 'dp')), may hold values from -0.25 to 0.25
- dec_up_bias: bfloat16 [2048], P(('pipe', 'dp')), may hold values from -1.25 to 1.25
- dec_down_weight: bfloat16 [2048, 512], P(('pipe', 'dp')), may hold values from -0.125 to 0.125
- cotangent: float32 [128, 588, 512], P('dp'), may hold values from -6 to 6
Outputs:
- band_means: float32 [6], P('pipe')
- band_variances: float32 [6], P('pipe')
- pixel_grad: float32 [128, 588, 1536], P('dp', None, 'pipe')
- patch_weight_grad: float32 [1536, 768], P(('pipe', 'dp'))
- patch_bias_grad: float32 [768], P(('pipe', 'dp'))
- enc_ln1_gain_grad: float32 [768], P(('pipe', 'dp'))
- enc_ln1_shift_grad: float32 [768], P(('pipe', 'dp'))
- enc_qkv_weight_grad: float32 [768, 2304], P(('pipe', 'dp'))
- enc_qv_bias_grad: float32 [1536], P(('pipe', 'dp'))
- enc_out_weight_grad: float32 [768, 768], P(('pipe', 'dp'))
- enc_out_bias_grad: float32 [768], P(('pipe', 'dp'))
- enc_ln2_gain_grad: float32 [768], P(('pipe', 'dp'))
- enc_ln2_shift_grad: float32 [768], P(('pipe', 'dp'))
- enc_up_weight_grad: float32 [768, 3072], P(('pipe', 'dp'))
- enc_up_bias_grad: float32 [3072], P(('pipe', 'dp'))
- enc_down_weight_grad: float32 [3072, 768], P(('pipe', 'dp'))
- enc_down_bias_grad: float32 [768], P(('pipe', 'dp'))
- dec_embed_weight_grad: float32 [768, 512], P(('pipe', 'dp'))
- dec_embed_bias_grad: float32 [512], P(('pipe', 'dp'))
- mask_token_grad: float32 [512], P(('pipe', 'dp'))
- dec_ln1_gain_grad: float32 [512], P(('pipe', 'dp'))
- dec_ln1_shift_grad: float32 [512], P(('pipe', 'dp'))
- dec_qkv_weight_grad: float32 [512, 1536], P(('pipe', 'dp'))
- dec_qv_bias_grad: float32 [1024], P(('pipe', 'dp'))
- dec_out_weight_grad: float32 [512, 512], P(('pipe', 'dp'))
- dec_out_bias_grad: float32 [512], P(('pipe', 'dp'))
- dec_ln2_gain_grad: float32 [512], P(('pipe', 'dp'))
- dec_ln2_shift_grad: float32 [512], P(('pipe', 'dp'))
- dec_up_weight_grad: float32 [512, 2048], P(('pipe', 'dp'))
- dec_up_bias_grad: float32 [2048], P(('pipe', 'dp'))
- dec_down_weight_grad: float32 [2048, 512], P(('pipe', 'dp'))
The draws below stay inside these ranges and needn't reach their ends.
Inputs may be any that keep to these rules, and one draw needn't show every extreme that they name: `visible_counts`: each item's number of visible patches; some item has exactly 235. `visible_index`: each row lists 235 distinct patch numbers; the first visible_counts of them are the item's visible patches, the rest name masked patches and are padding.
All inputs are finite; a program needn't handle non-finite values.
Results may differ from the reference program's by a relative error of at most 0.024.
Values may be sent and summed in bfloat16 or wider, within the bound.
No kernel may reach another device: no remote copies, remote signals or barrier semaphores. Data moves between devices by JAX's collectives and lax.ppermute only.
A program may use at most 384 MiB of HBM per device.

```python
import math
import jax
import jax.numpy as jnp
from jax import lax

D = 768
HEADS = 12
FF = 3072
DD = 512
DHEADS = 16
DFF = 2048
BANDS = 6
PATCHES = 588
PIX = 1536
VMAX = 235
ITEMS = 128
N_PIPE = 2


def draw_pixels(key, part):
    key = jax.random.fold_in(key, 11)
    base_key, offset_key, scale_key = jax.random.split(key, 3)
    draw_shape = (ITEMS, PATCHES, BANDS, PIX // BANDS)
    item_scale = 0.6 + 1.2 * jnp.arange(ITEMS).astype(jnp.float32) / max(ITEMS - 1, 1)
    offsets = jax.random.uniform(offset_key, (BANDS,), jnp.float32, -1.0, 1.0)
    base_values = jax.random.normal(base_key, draw_shape, jnp.float32)
    patch_scale = jnp.exp(jax.random.uniform(scale_key, (ITEMS, PATCHES, 1, 1), jnp.float32, -0.4, 0.4))
    values = base_values * patch_scale * item_scale[:, None, None, None] + offsets[None, None, :, None]
    return values.reshape(ITEMS, PATCHES, PIX)


def draw_visible_counts(key, part):
    key = jax.random.fold_in(key, 12)
    count_key, top_key = jax.random.split(key, 2)
    counts = jax.random.randint(count_key, (ITEMS,), PATCHES // 10, VMAX + 1)
    fullest = jax.random.randint(top_key, (), 0, ITEMS)
    counts = jnp.where(jnp.arange(ITEMS) == fullest, VMAX, counts)
    return counts.astype(jnp.int32)


def draw_visible_index(key, part):
    key = jax.random.fold_in(key, 13)
    item_keys = jax.random.split(key, ITEMS)

    def one_order(item_key):
        return jax.random.permutation(item_key, PATCHES)
    orders = jax.vmap(one_order)(item_keys)
    return orders[:, :VMAX].astype(jnp.int32)


def block_levels(stream_key, shape, cuts, smallest, largest):
    def one(axis_at, blocks):
        heights = jax.random.uniform(jax.random.fold_in(jax.random.fold_in(stream_key, 6), axis_at), (blocks,), jnp.float32, smallest / len(cuts), largest / len(cuts))
        return jnp.repeat(jnp.exp(heights), shape[axis_at] // blocks).reshape((-1,) + (1,) * (len(shape) - axis_at - 1))

    level = one(*cuts[0])
    for cut in cuts[1:]:
        level = level * one(*cut)
    return level


def scatter_about(key, dims, scale, limit, cuts=(), kind=jnp.bfloat16):
    array = scale * jax.random.normal(key, dims, jnp.float32)
    if cuts:
        array = array * block_levels(key, dims, cuts, -0.22, 0.18)
    return jnp.clip(array, -limit, limit).astype(kind)


def setup_inputs(seed: int = 0) -> dict:
    key_list = jax.random.split(jax.random.key(seed), 35)
    pixels = draw_pixels(jax.random.fold_in(key_list[34], 71), 0)
    visible_counts = draw_visible_counts(jax.random.fold_in(key_list[34], 71), 0)
    visible_index = draw_visible_index(jax.random.fold_in(key_list[34], 71), 0)
    running_mean = jnp.clip(jax.random.uniform(key_list[3], (BANDS,), jnp.float32, -1.0, 1.0) * block_levels(key_list[3], (BANDS,), ((0, 2),), -0.4, 0.0), -1.0, 1.0)
    running_var = jnp.clip(0.5 + 1.5 * jax.random.uniform(key_list[4], (BANDS,), jnp.float32) ** block_levels(key_list[4], (BANDS,), ((0, 2),), -0.2, 0.2), 0.5, 2.0)
    patch_weight = scatter_about(key_list[5], (PIX, D), PIX ** -0.5, 0.15625, ((0, 128),))
    patch_bias = scatter_about(key_list[6], (D,), 0.3, 1.75, ((0, 128),))
    enc_ln1_gain = jnp.clip(1.0 + 0.1 * jax.random.normal(key_list[7], (D,), jnp.float32), 0.5, 1.5).astype(jnp.bfloat16)
    enc_ln1_shift = scatter_about(key_list[8], (D,), 0.2, 1.25, ((0, 128),))
    enc_qkv_weight = scatter_about(key_list[9], (D, 3 * D), D ** -0.5, 0.21875, ((0, 128),))
    enc_qv_bias = scatter_about(key_list[10], (2 * D,), 0.2, 1.25, ((0, 128),))
    enc_out_weight = scatter_about(key_list[11], (D, D), (D // 16) ** -0.5, 0.875, ((0, 128),))
    enc_out_bias = scatter_about(key_list[12], (D,), 0.2, 1.25, ((0, 128),))
    enc_ln2_gain = jnp.clip(1.0 + 0.1 * jax.random.normal(key_list[13], (D,), jnp.float32), 0.5, 1.5).astype(jnp.bfloat16)
    enc_ln2_shift = scatter_about(key_list[14], (D,), 0.2, 1.25, ((0, 128),))
    enc_up_weight = scatter_about(key_list[15], (D, FF), D ** -0.5, 0.21875, ((0, 128),))
    enc_up_bias = scatter_about(key_list[16], (FF,), 0.2, 1.25, ((0, 128),))
    enc_down_weight = scatter_about(key_list[17], (FF, D), FF ** -0.5, 0.109375, ((0, 128),))
    enc_down_bias = scatter_about(key_list[18], (D,), 0.2, 1.25, ((0, 128),))
    dec_embed_weight = scatter_about(key_list[19], (D, DD), D ** -0.5, 0.21875, ((0, 128),))
    dec_embed_bias = scatter_about(key_list[20], (DD,), 0.3, 1.75, ((0, 128),))
    mask_token = scatter_about(key_list[21], (DD,), 1.0, 6.0, ((0, 128),))
    dec_ln1_gain = jnp.clip(1.0 + 0.1 * jax.random.normal(key_list[22], (DD,), jnp.float32), 0.5, 1.5).astype(jnp.bfloat16)
    dec_ln1_shift = scatter_about(key_list[23], (DD,), 0.2, 1.25, ((0, 128),))
    dec_qkv_weight = scatter_about(key_list[24], (DD, 3 * DD), DD ** -0.5, 0.25, ((0, 128),))
    dec_qv_bias = scatter_about(key_list[25], (2 * DD,), 0.2, 1.25, ((0, 128),))
    dec_out_weight = scatter_about(key_list[26], (DD, DD), (DD // 16) ** -0.5, 1.0, ((0, 128),))
    dec_out_bias = scatter_about(key_list[27], (DD,), 0.2, 1.25, ((0, 128),))
    dec_ln2_gain = jnp.clip(1.0 + 0.1 * jax.random.normal(key_list[28], (DD,), jnp.float32), 0.5, 1.5).astype(jnp.bfloat16)
    dec_ln2_shift = scatter_about(key_list[29], (DD,), 0.2, 1.25, ((0, 128),))
    dec_up_weight = scatter_about(key_list[30], (DD, DFF), DD ** -0.5, 0.25, ((0, 128),))
    dec_up_bias = scatter_about(key_list[31], (DFF,), 0.2, 1.25, ((0, 128),))
    dec_down_weight = scatter_about(key_list[32], (DFF, DD), DFF ** -0.5, 0.125, ((0, 128),))
    cotangent = scatter_about(key_list[33], (ITEMS, PATCHES, DD), 1.0, 6.0, ((0, 64),), jnp.float32)
    return dict(pixels=pixels, visible_counts=visible_counts, visible_index=visible_index, running_mean=running_mean, running_var=running_var, patch_weight=patch_weight, patch_bias=patch_bias, enc_ln1_gain=enc_ln1_gain, enc_ln1_shift=enc_ln1_shift, enc_qkv_weight=enc_qkv_weight, enc_qv_bias=enc_qv_bias, enc_out_weight=enc_out_weight, enc_out_bias=enc_out_bias, enc_ln2_gain=enc_ln2_gain, enc_ln2_shift=enc_ln2_shift, enc_up_weight=enc_up_weight, enc_up_bias=enc_up_bias, enc_down_weight=enc_down_weight, enc_down_bias=enc_down_bias, dec_embed_weight=dec_embed_weight, dec_embed_bias=dec_embed_bias, mask_token=mask_token, dec_ln1_gain=dec_ln1_gain, dec_ln1_shift=dec_ln1_shift, dec_qkv_weight=dec_qkv_weight, dec_qv_bias=dec_qv_bias, dec_out_weight=dec_out_weight, dec_out_bias=dec_out_bias, dec_ln2_gain=dec_ln2_gain, dec_ln2_shift=dec_ln2_shift, dec_up_weight=dec_up_weight, dec_up_bias=dec_up_bias, dec_down_weight=dec_down_weight, cotangent=cotangent)


@jax.custom_vjp
def low(v):
    return lax.optimization_barrier(v.astype(jnp.bfloat16)).astype(jnp.float32)

@jax.custom_vjp
def low_back(v):
    return v

def low_keep(v):
    return (low(v), None)

def low_pass(kept, grad):
    return (grad,)

def back_keep(v):
    return (v, None)

def back_low(kept, grad):
    return (low(grad),)
low.defvjp(low_keep, low_pass)
low_back.defvjp(back_keep, back_low)
band_epsilon = 1e-05
norm_epsilon = 1e-06
masked_score = -1e+30

def matmul(left, right):
    return jnp.dot(left, right, precision=lax.Precision.HIGHEST)

def layer_norm(residual, gain, shift):
    center = residual - lax.optimization_barrier(jnp.mean(residual, axis=-1, keepdims=True))
    spread = lax.optimization_barrier(jnp.mean(center * center, axis=-1, keepdims=True))
    return center * lax.rsqrt(spread + norm_epsilon) * gain + shift

def position_table(length, model_width):
    half_width = model_width // 2
    place_ids = jnp.arange(length).astype(jnp.float32)[:, None]
    freq_rate = jnp.exp(jnp.arange(half_width).astype(jnp.float32) * (-math.log(10000.0) / half_width))
    phase_angle = place_ids * freq_rate[None, :]
    return jnp.concatenate([jnp.sin(phase_angle), jnp.cos(phase_angle)], axis=1)

def block(residual, weights, head_count, key_keep):
    norm_gain, norm_shift, qkv_weight, qv_bias, out_weight, out_bias, mlp_gain, mlp_shift, up_weight, up_bias, down_weight, down_bias = weights
    length, model_width = residual.shape
    head_size = model_width // head_count
    normed = low(layer_norm(residual, norm_gain, norm_shift))
    qkv_bias = jnp.concatenate([qv_bias[:model_width], jnp.zeros((model_width,), jnp.float32), qv_bias[model_width:]])
    qkv_rows = low_back(low(matmul(normed, qkv_weight) + qkv_bias))
    queries = qkv_rows[:, :model_width].reshape(length, head_count, head_size)
    key_rows = qkv_rows[:, model_width:2 * model_width].reshape(length, head_count, head_size)
    values = qkv_rows[:, 2 * model_width:].reshape(length, head_count, head_size)
    scores = jnp.einsum('qhd,khd->hqk', queries, key_rows, precision=lax.Precision.HIGHEST) * head_size ** (-0.5)
    scores = low_back(jnp.where(key_keep[None, None, :], scores, masked_score))
    prob_table = low(jax.nn.softmax(scores, axis=-1))
    attended = jnp.einsum('hqk,khd->qhd', prob_table, values, precision=lax.Precision.HIGHEST).reshape(length, model_width)
    attended = low_back(low(attended))
    hidden = residual + low_back(matmul(attended, out_weight) + out_bias)
    second = low(layer_norm(hidden, mlp_gain, mlp_shift))
    up_proj = low_back(matmul(second, up_weight) + up_bias)
    active = low(jax.nn.gelu(up_proj))
    return hidden + low_back(matmul(active, down_weight) + down_bias)

def item_forward(params, normed, item_index, item_count):
    patch_weight, patch_bias, encoder, embed_weight, embed_bias, mask_token, decoder = params
    slot_ids = jnp.arange(VMAX)
    key_keep = slot_ids < item_count
    picked = low_back(low(normed[item_index]))
    pieces = picked.reshape(VMAX, N_PIPE, PIX // N_PIPE)
    weight_parts = patch_weight.reshape(N_PIPE, PIX // N_PIPE, D)
    embedded = low(jnp.einsum('vph,phd->pvd', pieces, weight_parts, precision=lax.Precision.HIGHEST))
    start_rows = low_back(embedded[0] + embedded[1] + patch_bias + position_table(PATCHES, D)[item_index])
    encoded = low_back(low(block(start_rows, encoder, HEADS, key_keep)))
    latent = low_back(low(matmul(encoded, embed_weight) + embed_bias))
    onehot = ((item_index[:, None] == jnp.arange(PATCHES)[None, :]) & key_keep[:, None]).astype(jnp.float32)
    covered = lax.optimization_barrier(jnp.sum(onehot, axis=0))
    full_grid = matmul(onehot.T, latent) + (1.0 - covered)[:, None] * mask_token + position_table(PATCHES, DD)
    return block(full_grid, decoder, DHEADS, jnp.ones((PATCHES,), dtype=bool))

def reference(pixels, visible_counts, visible_index, running_mean, running_var, patch_weight, patch_bias, enc_ln1_gain, enc_ln1_shift, enc_qkv_weight, enc_qv_bias, enc_out_weight, enc_out_bias, enc_ln2_gain, enc_ln2_shift, enc_up_weight, enc_up_bias, enc_down_weight, enc_down_bias, dec_embed_weight, dec_embed_bias, mask_token, dec_ln1_gain, dec_ln1_shift, dec_qkv_weight, dec_qv_bias, dec_out_weight, dec_out_bias, dec_ln2_gain, dec_ln2_shift, dec_up_weight, dec_up_bias, dec_down_weight, cotangent):
    band_view = pixels.reshape(ITEMS, PATCHES, BANDS, PIX // BANDS)
    population = ITEMS * PATCHES * (PIX // BANDS)
    band_mean = lax.optimization_barrier(jnp.sum(band_view, axis=(0, 1, 3))) / population
    band_square = lax.optimization_barrier(jnp.sum(band_view * band_view, axis=(0, 1, 3))) / population
    band_var = band_square - band_mean * band_mean
    band_scale = lax.rsqrt(band_var + band_epsilon)
    normed = ((band_view - band_mean[:, None]) * band_scale[:, None]).reshape(ITEMS, PATCHES, PIX)
    band_means = 0.9 * running_mean + 0.1 * band_mean
    band_variances = 0.9 * running_var + 0.1 * band_var
    encoder = tuple((piece.astype(jnp.float32) for piece in (enc_ln1_gain, enc_ln1_shift, enc_qkv_weight, enc_qv_bias, enc_out_weight, enc_out_bias, enc_ln2_gain, enc_ln2_shift, enc_up_weight, enc_up_bias, enc_down_weight, enc_down_bias)))
    decoder = tuple((piece.astype(jnp.float32) for piece in (dec_ln1_gain, dec_ln1_shift, dec_qkv_weight, dec_qv_bias, dec_out_weight, dec_out_bias, dec_ln2_gain, dec_ln2_shift, dec_up_weight, dec_up_bias, dec_down_weight)))
    params = (patch_weight.astype(jnp.float32), patch_bias.astype(jnp.float32), encoder, dec_embed_weight.astype(jnp.float32), dec_embed_bias.astype(jnp.float32), mask_token.astype(jnp.float32), decoder)

    def forward(normed_in, params_in):
        full_params = params_in[:6] + (tuple(params_in[6]) + (jnp.zeros((DD,), jnp.float32),),)

        def one_item(packed):
            return item_forward(full_params, packed[0], packed[1], packed[2])
        return lax.map(jax.checkpoint(one_item), (normed_in, visible_index, visible_counts))
    decoded, pull_back = jax.vjp(forward, normed, params)
    normed_grad, param_grads = pull_back(cotangent)
    pixel_grad = (normed_grad.reshape(ITEMS, PATCHES, BANDS, PIX // BANDS) * band_scale[:, None]).reshape(ITEMS, PATCHES, PIX)
    enc_grads = param_grads[2]
    dec_grads = param_grads[6]
    return (band_means, band_variances, pixel_grad, param_grads[0], param_grads[1], enc_grads[0], enc_grads[1], enc_grads[2], enc_grads[3], enc_grads[4], enc_grads[5], enc_grads[6], enc_grads[7], enc_grads[8], enc_grads[9], enc_grads[10], enc_grads[11], param_grads[3], param_grads[4], param_grads[5], dec_grads[0], dec_grads[1], dec_grads[2], dec_grads[3], dec_grads[4], dec_grads[5], dec_grads[6], dec_grads[7], dec_grads[8], dec_grads[9], dec_grads[10])
```

```python
import functools
import math

import jax
import jax.numpy as jnp
from jax import lax
from jax.experimental import pallas as pl
from jax.experimental.pallas import tpu as pltpu
from jax.sharding import Mesh
from jax.sharding import PartitionSpec as P

HEADS = 12
DHEADS = 16
SLOTS = 256
GRID = 592

band_epsilon = 1e-05
norm_epsilon = 1e-06
masked_score = -1e30

PIPE = ("z_lo",)
DP = ("x", "z_hi", "y", "core")
ALL = PIPE + DP
RING = {"x": ("x",), "y": ("y",), "z": ("z_lo", "z_hi")}
F32 = jnp.float32
BF16 = jnp.bfloat16


def along(axis, place):
    return (place % 2) * 2 + place // 2 if axis == "z" else place


def ring_place(axis):
    if axis == "z":
        return lax.axis_index("z_hi") * 2 + lax.axis_index("z_lo")
    return lax.axis_index(axis)


def shift(value, axis, step, mirrored):
    pairs = []
    for place in range(4):
        for core in range(2):
            target = (place + (-step if mirrored and core else step)) % 4
            pairs.append((along(axis, place) * 2 + core, along(axis, target) * 2 + core))
    return lax.ppermute(value, RING[axis] + ("core",), pairs)


def swap(value, axis):
    return lax.ppermute(value, axis, [(0, 1), (1, 0)])


def put(blocks, block, index):
    return lax.dynamic_update_slice_in_dim(blocks, block[None], index, axis=0)


def take(blocks, index):
    return lax.dynamic_index_in_dim(blocks, index, axis=0, keepdims=False)


def direction():
    return jnp.where(lax.axis_index("core") == 0, 1, 3)


def gather_small(block, axis):
    me = ring_place(axis)
    blocks = put(jnp.zeros((4,) + block.shape, block.dtype), block, along(axis, me))
    for step in (1, 2, 3):
        blocks = put(blocks, shift(block, axis, step, False), along(axis, (me + 4 - step) % 4))
    return blocks


def gather_large(block, axis):
    me, way = ring_place(axis), direction()
    blocks = put(jnp.zeros((4,) + block.shape, block.dtype), block, along(axis, me))
    for step in (1, 2, 3):
        block = shift(block, axis, 1, True)
        blocks = put(blocks, block, along(axis, (me + (4 - way) * step) % 4))
    return blocks


def scatter_small(blocks, axis):
    me = ring_place(axis)
    total = take(blocks, along(axis, me)).astype(F32)
    for step in (1, 2, 3):
        sent = take(blocks, along(axis, (me + step) % 4))
        total = total + shift(sent, axis, step, False).astype(F32)
    return total.astype(BF16)


def scatter_large(blocks, axis):
    me, way = ring_place(axis), direction()
    part = take(blocks, along(axis, (me + 4 - way) % 4))
    for step in (1, 2, 3):
        part = shift(part, axis, 1, True)
        own = take(blocks, along(axis, (me + (4 - way) * (step + 1)) % 4))
        part = (part.astype(F32) + own.astype(F32)).astype(BF16)
    return part


def by_core(mine, other):
    first = lax.axis_index("core") == 0
    return jnp.where(first, mine, other), jnp.where(first, other, mine)


def halves(array):
    rows, columns = array.shape
    return array.reshape(rows, 2, columns // 2).transpose(1, 0, 2)


def chunks(array, width):
    *lead, rows, columns = array.shape
    count = columns // width
    cut = jnp.moveaxis(array.reshape(*lead, rows, count, width), -2, -3)
    return cut.reshape(*lead, count * rows, width)


def unchunks(array, rows):
    *lead, total, width = array.shape
    count = total // rows
    cut = jnp.moveaxis(array.reshape(*lead, count, rows, width), -3, -2)
    return cut.reshape(*lead, rows, count * width)


def natural(array, order):
    rows, width = array.shape[-2:]
    dims = []
    for axis in order:
        dims.extend((2, 2) if axis == "z" else (4,))
    names = []
    for axis in order:
        names.extend(("zl", "zh") if axis == "z" else (axis,))
    array = array.reshape(*dims, rows, width)
    wanted = [n for n in ("zl", "x", "zh", "y") if n in names]
    perm = [names.index(n) for n in wanted] + [len(names), len(names) + 1]
    return array.transpose(perm).reshape(-1, width)


def unnatural(array, order, rows):
    names = []
    for axis in order:
        names.extend(("zl", "zh") if axis == "z" else (axis,))
    wanted = [n for n in ("zl", "x", "zh", "y") if n in names]
    size = {"zl": 2, "zh": 2, "x": 4, "y": 4}
    width = array.shape[-1]
    array = array.reshape(*[size[n] for n in wanted], rows, width)
    perm = [wanted.index(n) for n in names] + [len(names), len(names) + 1]
    array = array.transpose(perm)
    return array.reshape(*([4] * len(order)), rows, width)


def pad_rows(array, rows):
    return jnp.pad(array, ((0, rows - array.shape[0]), (0, 0)))


def gather_weights(enc6, enc_up, enc_down, dec4, dec_up, dec_down, patch, vector):
    core = lax.axis_index("core")

    def cut(array):
        both = halves(array)
        return take(both, core), take(both, 1 - core)

    keep, give = [], []
    for pieces in ((enc6, enc_up), (dec4, dec_up)):
        kept, given = zip(*[cut(piece) for piece in pieces])
        keep.append(pad_rows(jnp.concatenate(kept, axis=1), 8))
        give.append(pad_rows(jnp.concatenate(given, axis=1), 8))
    keep_ab, give_ab = jnp.concatenate(keep, axis=1), jnp.concatenate(give, axis=1)
    kept, given = zip(*[cut(piece) for piece in (enc_down, dec_down, patch, pad_rows(vector, 4))])
    keep_c = jnp.concatenate([chunks(k, 128) for k in kept], axis=0)
    give_c = jnp.concatenate([chunks(g, 128) for g in given], axis=0)
    ab = jnp.stack(by_core(keep_ab, swap(give_ab, "core")))
    pair_c = jnp.stack(by_core(keep_c, swap(give_c, "core")))
    part_c, at = [], 0
    for total, rows in ((72, 24), (32, 16), (36, 12), (4, 4)):
        piece = pair_c[:, at : at + total].reshape(2, total // rows, rows, 128)
        part_c.append(piece.transpose(1, 0, 2, 3).reshape(2 * total, 128))
        at += total
    gap = jnp.zeros((16, 128), BF16)
    part_c = jnp.concatenate([part_c[0], gap, part_c[1], gap, part_c[2], part_c[3]], axis=0)

    ab = gather_small(ab, "y")
    wide_e = enc6.shape[1] // 2
    wide_d = dec4.shape[1] // 2
    edge = wide_e + enc_up.shape[1] // 2
    enc_ab = ab[:, :, :6, :edge].reshape(48, edge)
    dec_ab = ab[:, :, :4, edge:].reshape(32, -1)
    part_a = jnp.concatenate(
        [chunks(dec_ab[:, :wide_d], 256), jnp.zeros((16, 256), BF16), chunks(enc_ab[:, :wide_e], 256)], axis=0)
    part_b = jnp.concatenate([chunks(enc_ab[:, wide_e:], 256), chunks(dec_ab[:, wide_d:], 256)], axis=0)

    part_a = gather_small(part_a, "z")
    part_b = gather_small(part_b, "x")
    part_c = gather_small(part_c, "x")
    part_c = gather_small(part_c, "z")
    part_a = gather_large(part_a, "x")
    part_b = gather_large(part_b, "z")
    part_c = gather_large(part_c, "y")
    return unpack_a(part_a), unpack_b(part_b), unpack_c(part_c)


def core_id():
    return lax.axis_index("core").astype(jnp.int32).reshape(1)


def on_each_core(core_ref, mine, other, work):
    @pl.when(core_ref[0] == 0)
    def _():
        work((mine, other))

    @pl.when(core_ref[0] != 0)
    def _():
        work((other, mine))


def unpack_call(kernel, part, block, index, outs, out_blocks):
    return pl.pallas_call(
        kernel,
        out_shape=outs,
        grid_spec=pltpu.PrefetchScalarGridSpec(
            num_scalar_prefetch=1,
            grid=(2, 4),
            in_specs=[pl.BlockSpec(block, index)] * 2,
            out_specs=[pl.BlockSpec(b, lambda zl, x, c: (zl * 4 + x, 0)) for b in out_blocks],
        ),
        compiler_params=pltpu.CompilerParams(vmem_limit_bytes=40 << 20),
    )(core_id(), part, swap(part, "core"))


def unpack_a_kernel(core_ref, mine, other, qkv, out, embed, dqkv, dout):
    def work(sides):
        for zh in range(2):
            for j in range(14):
                value = sides[j // 7][0, 0, zh, 144 + j % 7 * 48 : 192 + j % 7 * 48, :]
                target, at = (qkv, j) if j < 9 else (out, j - 9) if j < 12 else (embed, j - 12)
                target[zh * 48 : zh * 48 + 48, at * 256 : at * 256 + 256] = value
            for j in range(8):
                value = sides[j // 4][0, 0, zh, j % 4 * 32 : 32 + j % 4 * 32, :]
                target, at = (dqkv, j) if j < 6 else (dout, j - 6)
                target[zh * 32 : zh * 32 + 32, at * 256 : at * 256 + 256] = value

    on_each_core(core_ref, mine, other, work)


def unpack_a(part):
    outs = [(768, 2304), (768, 768), (768, 512), (512, 1536), (512, 512)]
    part = part.reshape(4, 2, 2, 480, 256)
    return unpack_call(
        unpack_a_kernel, part, (1, 1, 2, 480, 256), lambda zl, x, c: (x, zl, 0, 0, 0),
        [jax.ShapeDtypeStruct(o, BF16) for o in outs], [(o[0] // 8, o[1]) for o in outs])


def unpack_b_kernel(core_ref, mine, other, up, dup):
    def work(sides):
        for zh in range(2):
            for j in range(12):
                value = sides[j // 6][0, zh, 0, j % 6 * 48 : 48 + j % 6 * 48, :]
                up[zh * 48 : zh * 48 + 48, j * 256 : j * 256 + 256] = value
            for j in range(8):
                value = sides[j // 4][0, zh, 0, 288 + j % 4 * 32 : 320 + j % 4 * 32, :]
                dup[zh * 32 : zh * 32 + 32, j * 256 : j * 256 + 256] = value

    on_each_core(core_ref, mine, other, work)


def unpack_b(part):
    outs = [(768, 3072), (512, 2048)]
    part = part.reshape(2, 2, 4, 416, 256)
    return unpack_call(
        unpack_b_kernel, part, (1, 2, 1, 416, 256), lambda zl, x, c: (zl, 0, x, 0, 0),
        [jax.ShapeDtypeStruct(o, BF16) for o in outs], [(o[0] // 8, o[1]) for o in outs])


def unpack_c_kernel(core_ref, mine, other, down, ddown, patch, vector):
    def work(sides):
        for side in range(2):
            ref = sides[side]
            small = [ref[y, 0, zh, 0, 240:320, :].astype(F32) for zh in range(2) for y in range(4)]
            for k in range(8):
                zh, y = k // 4, k % 4
                for j in range(3):
                    at = side * 384 + j * 128
                    down[k * 48 : k * 48 + 48, at : at + 128] = ref[y, 0, zh, 0, j * 48 : j * 48 + 48, :]
                for j in range(2):
                    at = side * 256 + j * 128
                    ddown[k * 32 : k * 32 + 32, at : at + 128] = ref[y, 0, zh, 0, 160 + j * 32 : 192 + j * 32, :]
            for j in range(3):
                at = side * 384 + j * 128
                rows = jnp.concatenate([s[j * 24 : j * 24 + 24] for s in small], axis=0)
                patch[:, at : at + 128] = rows.astype(BF16)
            for k in range(8):
                vector[2 * k : 2 * k + 1, side * 128 : side * 128 + 128] = small[k][72:73]
                vector[2 * k + 1 : 2 * k + 2, side * 128 : side * 128 + 128] = small[k][76:77]

    on_each_core(core_ref, mine, other, work)


def unpack_c(part):
    outs = [(3072, 768, BF16), (2048, 512, BF16), (1536, 768, BF16), (128, 256, F32)]
    part = part.reshape(4, 2, 2, 4, 320, 128)
    return unpack_call(
        unpack_c_kernel, part, (4, 1, 2, 1, 320, 128), lambda zl, x, c: (0, zl, 0, x, 0, 0),
        [jax.ShapeDtypeStruct(o[:2], o[2]) for o in outs], [(o[0] // 8, o[1]) for o in outs])


def wide_grad_kernel(order, rows, lhs, rhs, *rest):
    out, turned = rest[-2:]

    @pl.when(pl.program_id(0) == 0)
    def _():
        turned[...] = lhs[...].T

    result = jnp.dot(turned[...], rhs[0], preferred_element_type=F32).astype(BF16)
    for block in range(16):
        zl, x, zh = block // 8, block // 2 % 4, block % 2
        spot = (0, x, zl, zh) if order == "xz" else (0, zl, zh, x)
        out[spot] = result[block * rows : block * rows + rows]


def wide_grad(lhs, rhs, buffer, shape, order, rows, row_block, first, per_side):
    length, height = lhs.shape
    parts, _, width = rhs.shape
    per_part = width // 256
    block = (1, 4, 2, 2, rows, 256) if order == "xz" else (1, 2, 2, 4, rows, 256)

    def place(j):
        chunk = j + first
        return (chunk // per_side, 0, 0, 0, row_block + chunk % per_side, 0)

    given = () if buffer is None else (buffer,)
    return pl.pallas_call(
        functools.partial(wide_grad_kernel, order, rows),
        out_shape=jax.ShapeDtypeStruct(shape, BF16),
        grid=(parts * per_part,),
        in_specs=[
            pl.BlockSpec((length, height), lambda j: (0, 0)),
            pl.BlockSpec((1, length, 256), lambda j: (j // per_part, 0, j % per_part)),
        ] + [pl.BlockSpec(memory_space=pl.ANY)] * len(given),
        out_specs=pl.BlockSpec(block, place),
        scratch_shapes=[pltpu.VMEM((height, length), BF16)],
        input_output_aliases={2: 0} if given else {},
        compiler_params=pltpu.CompilerParams(vmem_limit_bytes=40 << 20),
        cost_estimate=pl.CostEstimate(
            flops=2 * length * height * width * parts, transcendentals=0,
            bytes_accessed=2 * (length * height + parts * length * width + parts * height * width)),
    )(lhs, rhs, *given)


def tall_grad_kernel(rows, pipe_ref, lhs, rhs, *rest):
    out = rest[-1]
    result = lax.dot_general(lhs[...], rhs[...], (((0,), (0,)), ((), ())), preferred_element_type=F32)
    if rows == 24:
        result = jnp.where(pl.program_id(1) // 2 == pipe_ref[0], result, 0.0)
        for xs in range(2):
            for zh in range(2):
                for y in range(4):
                    k = ((xs * 2 + zh) * 4 + y) * 24
                    pieces = [result[k : k + 24, j * 128 : j * 128 + 128] for j in range(3)]
                    pieces.append(jnp.zeros((8, 128), F32))
                    out[0, y, 0, zh, xs, :, :] = jnp.concatenate(pieces, axis=0).astype(BF16)
        return
    result = result.astype(BF16)
    for xs in range(2):
        for zh in range(2):
            for y in range(4):
                k = ((xs * 2 + zh) * 4 + y) * rows
                for j in range(result.shape[1] // 128):
                    out[0, y, 0, zh, xs, j * rows : j * rows + rows, :] = (
                        result[k : k + rows, j * 128 : j * 128 + 128])


def tall_grad(lhs, rhs, buffer, rows, row_block, pipe, split):
    length, height = lhs.shape
    side = rhs.shape[1] // 2 // split
    tile = 16 * rows
    count = side // 128 * rows + (8 if rows == 24 else 0)
    shape = (2, 4, 2, 2, 4, 320, 128)
    given = () if buffer is None else (buffer,)
    turns = 2 if rows == 24 else 4
    return pl.pallas_call(
        functools.partial(tall_grad_kernel, rows),
        out_shape=jax.ShapeDtypeStruct(shape, BF16),
        grid_spec=pltpu.PrefetchScalarGridSpec(
            num_scalar_prefetch=1,
            grid=(2, 4, split),
            in_specs=[
                pl.BlockSpec((length, tile), lambda h, t, s, p: (0, t % turns)),
                pl.BlockSpec((length, side), lambda h, t, s, p: (0, h * split + s)),
            ] + [pl.BlockSpec(memory_space=pl.ANY)] * len(given),
            out_specs=pl.BlockSpec(
                (1, 4, 1, 2, 2, count, 128), lambda h, t, s, p: (h, 0, t // 2, 0, t % 2, row_block + s, 0)),
        ),
        input_output_aliases={3: 0} if given else {},
        compiler_params=pltpu.CompilerParams(vmem_limit_bytes=40 << 20),
        cost_estimate=pl.CostEstimate(
            flops=2 * length * height * rhs.shape[1], transcendentals=0,
            bytes_accessed=4 * height * rhs.shape[1]),
    )(pipe, lhs, rhs, *given)


def scatter_grads(part_a, part_b, part_c, wide_e, wide_up, wide_d):
    core = lax.axis_index("core")

    def pair(part):
        got = swap(take(part, 1 - core), "core")
        return (take(part, core).astype(F32) + got.astype(F32)).astype(BF16)

    part_a, part_b, part_c = pair(part_a), pair(part_b), pair(part_c)
    part_a = part_a.reshape(4, 4, 480, 256)
    part_b = part_b.reshape(4, 4, 416, 256)
    part_c = part_c.reshape(4, 4, 4, 320, 128)
    part_a = scatter_large(part_a, "x")
    part_b = scatter_large(part_b, "z")
    part_c = scatter_large(part_c, "y")
    part_a = scatter_small(part_a, "z")
    part_b = scatter_small(part_b, "x")
    part_c = scatter_small(part_c, "z")
    part_c = scatter_small(part_c, "x")
    edge = wide_e + wide_up
    enc_ab = jnp.concatenate([unchunks(part_a[144:], 48), unchunks(part_b[:288], 48)], axis=1)
    dec_ab = jnp.concatenate([unchunks(part_a[:128], 32), unchunks(part_b[288:], 32)], axis=1)
    enc_ab = jnp.pad(enc_ab.reshape(4, 2, 6, edge), ((0, 0), (0, 0), (0, 2), (0, 0)))
    dec_ab = jnp.pad(dec_ab.reshape(4, 2, 4, -1), ((0, 0), (0, 0), (0, 4), (0, 0)))
    ab = scatter_small(jnp.concatenate([enc_ab, dec_ab], axis=-1), "y")

    def finish(pair):
        got = swap(take(pair, 1 - core), "core")
        return by_core(take(pair, core), got)

    low, high = finish(ab)

    def columns(first, last, rows):
        return jnp.concatenate([low[:rows, first:last], high[:rows, first:last]], axis=1).astype(F32)

    out6 = columns(0, wide_e, 6)
    out_up = columns(wide_e, edge, 6)
    out4 = columns(edge, edge + wide_d, 4)
    out_dup = columns(edge + wide_d, low.shape[1], 4)
    pieces = []
    for at, total, rows in ((0, 144, 24), (160, 64, 16), (240, 72, 12), (312, 8, 4)):
        piece = part_c[at : at + total].reshape(total // (2 * rows), 2, rows, 128)
        pieces.append(piece.transpose(1, 0, 2, 3).reshape(2, total // 2, 128))
    low, high = finish(jnp.concatenate(pieces, axis=1))
    outs, at = [], 0
    for total, rows in ((72, 24), (32, 16), (36, 12), (4, 4)):
        both = [unchunks(side[at : at + total], rows) for side in (low, high)]
        outs.append(jnp.concatenate(both, axis=1).astype(F32))
        at += total
    return out6, out_up, outs[0], out4, out_dup, outs[1], outs[2], outs[3][0]


def layer_norm(residual, gain, shift_row):
    center = residual - jnp.mean(residual, axis=-1, keepdims=True)
    spread = jnp.mean(center * center, axis=-1, keepdims=True)
    return center * lax.rsqrt(spread + norm_epsilon) * gain + shift_row


def frequencies(model_width):
    half_width = model_width // 2
    return jnp.exp(jnp.arange(half_width).astype(F32) * (-math.log(10000.0) / half_width))


def position_rows(places, model_width):
    phase_angle = places.astype(F32)[:, None] * frequencies(model_width)[None, :]
    return jnp.concatenate([jnp.sin(phase_angle), jnp.cos(phase_angle)], axis=1)


def dot(left, right):
    return jnp.dot(left, right, preferred_element_type=F32)


def dot_t(left, right):
    return lax.dot_general(left, right, (((1,), (1,)), ((), ())), preferred_element_type=F32)


def t_dot(left, right):
    return lax.dot_general(left, right, (((0,), (0,)), ((), ())), preferred_element_type=F32)


def attend_kernel(size, count_ref, q_ref, k_ref, v_ref, o_ref):
    length = q_ref.shape[0]
    q, k, v = q_ref[...], k_ref[...], v_ref[...]
    kept = lax.broadcasted_iota(jnp.int32, (1, length), 1) < count_ref[0]
    lane = lax.broadcasted_iota(jnp.int32, (1, 128), 1)
    total = jnp.zeros((length, 128), F32)
    for head in range(128 // size):
        mine = (lane >= head * size) & (lane < (head + 1) * size)
        scores = dot_t(jnp.where(mine, q, jnp.zeros_like(q)), k)
        scores = jnp.where(kept, scores * size ** (-0.5), masked_score)
        weight = jnp.exp(scores - jnp.max(scores, axis=1, keepdims=True))
        prob = (weight * (1.0 / jnp.sum(weight, axis=1, keepdims=True))).astype(BF16)
        total = total + dot(prob, jnp.where(mine, v, jnp.zeros_like(v)))
    o_ref[...] = total.astype(BF16)

def attend(qkv, heads, count):
    length, width = qkv.shape[0], qkv.shape[1] // 3
    groups = width // 128
    spec = lambda part: pl.BlockSpec((length, 128), lambda g, c, part=part: (0, part * groups + g))
    return pl.pallas_call(
        functools.partial(attend_kernel, width // heads),
        out_shape=jax.ShapeDtypeStruct((length, width), BF16),
        grid_spec=pltpu.PrefetchScalarGridSpec(
            num_scalar_prefetch=1, grid=(groups,),
            in_specs=[spec(0), spec(1), spec(2)],
            out_specs=pl.BlockSpec((length, 128), lambda g, c: (0, g))),
        compiler_params=pltpu.CompilerParams(vmem_limit_bytes=48 << 20),
    )(count, qkv, qkv, qkv)

def attend_back_kernel(size, count_ref, q_ref, k_ref, v_ref, g_ref, o_ref):
    length = q_ref.shape[0]
    q, k, v, g = q_ref[...], k_ref[...], v_ref[...], g_ref[...]
    kept = lax.broadcasted_iota(jnp.int32, (length, 1), 0) < count_ref[0]
    lane = lax.broadcasted_iota(jnp.int32, (1, 128), 1)
    dq = jnp.zeros((length, 128), F32)
    dk = jnp.zeros((length, 128), F32)
    dv = jnp.zeros((length, 128), F32)
    zero = jnp.zeros_like(q)
    for head in range(128 // size):
        mine = (lane >= head * size) & (lane < (head + 1) * size)
        q_h, k_h, g_h = jnp.where(mine, q, zero), jnp.where(mine, k, zero), jnp.where(mine, g, zero)
        scores = dot_t(k, q_h)
        scores = jnp.where(kept, scores * size ** (-0.5), masked_score)
        weight = jnp.exp(scores - jnp.max(scores, axis=0, keepdims=True))
        prob = weight * (1.0 / jnp.sum(weight, axis=0, keepdims=True))
        dv = dv + dot(prob.astype(BF16), g_h)
        prob_grad = dot_t(v, g_h)
        inner = jnp.sum(prob * prob_grad, axis=0, keepdims=True)
        score_grad = (prob * (prob_grad - inner)).astype(BF16)
        dk = dk + dot(score_grad, q_h)
        dq = dq + t_dot(score_grad, k_h)
    o_ref[0] = (dq * size ** (-0.5)).astype(BF16)
    o_ref[1] = (dk * size ** (-0.5)).astype(BF16)
    o_ref[2] = dv.astype(BF16)

def attend_back(qkv, grad, heads, count):
    length, width = qkv.shape[0], qkv.shape[1] // 3
    groups = width // 128
    spec = lambda part: pl.BlockSpec((length, 128), lambda g, c, part=part: (0, part * groups + g))
    return pl.pallas_call(
        functools.partial(attend_back_kernel, width // heads),
        out_shape=jax.ShapeDtypeStruct((3, length, width), BF16),
        grid_spec=pltpu.PrefetchScalarGridSpec(
            num_scalar_prefetch=1, grid=(groups,),
            in_specs=[spec(0), spec(1), spec(2), spec(0)],
            out_specs=pl.BlockSpec((3, length, 128), lambda g, c: (0, 0, g))),
        compiler_params=pltpu.CompilerParams(vmem_limit_bytes=56 << 20),
    )(count, qkv, qkv, qkv, grad)


def block_forward(residual, weights, head_count, key_keep):
    (gain1, shift1, qkv_weight, qv_bias, out_weight, out_bias, gain2, shift2, up_weight, up_bias,
     down_weight, down_bias) = weights
    width = residual.shape[1]
    normed = layer_norm(residual, gain1, shift1).astype(BF16)
    qkv_bias = jnp.concatenate([qv_bias[:width], jnp.zeros((width,), F32), qv_bias[width:]])
    qkv_rows = (dot(normed, qkv_weight) + qkv_bias).astype(BF16)
    attended = attend(qkv_rows, head_count, key_keep)
    hidden = residual + (dot(attended, out_weight) + out_bias)
    second = layer_norm(hidden, gain2, shift2).astype(BF16)
    up_proj = dot(second, up_weight) + up_bias
    active = jax.nn.gelu(up_proj).astype(BF16)
    stored = (residual, normed, qkv_rows, attended, hidden, second, up_proj, active)
    return hidden, active, stored


def block_backward(grad_out, stored, weights, head_count, key_keep):
    (gain1, shift1, qkv_weight, qv_bias, out_weight, out_bias, gain2, shift2, up_weight, up_bias,
     down_weight, down_bias) = weights
    (residual, normed, qkv_rows, attended, hidden, second, up_proj, active) = stored
    width = residual.shape[1]
    down_branch = grad_out.astype(BF16)
    down_bias_grad = jnp.sum(down_branch.astype(F32), axis=0)
    down_weight_grad = (active, down_branch)
    active_grad = dot_t(down_branch, down_weight)
    up_grad = jax.vjp(jax.nn.gelu, up_proj)[1](active_grad)[0].astype(BF16)
    up_bias_grad = jnp.sum(up_grad.astype(F32), axis=0)
    up_weight_grad = (second, up_grad[None])
    second_grad = dot_t(up_grad, up_weight)
    hidden_grad, gain2_grad, shift2_grad = jax.vjp(layer_norm, hidden, gain2, shift2)[1](second_grad)
    hidden_grad = hidden_grad + grad_out
    attn_branch = hidden_grad.astype(BF16)
    out_bias_grad = jnp.sum(attn_branch.astype(F32), axis=0)
    out_weight_grad = (attended, attn_branch[None])
    attended_grad = dot_t(attn_branch, out_weight).astype(BF16)
    qkv_parts = attend_back(qkv_rows, attended_grad, head_count, key_keep)
    qkv_grad = jnp.concatenate([qkv_parts[0], qkv_parts[1], qkv_parts[2]], axis=1)
    qkv_sums = jnp.sum(qkv_grad.astype(F32), axis=0)
    qv_bias_grad = jnp.concatenate([qkv_sums[:width], qkv_sums[2 * width :]])
    qkv_weight_grad = (normed, qkv_parts)
    normed_grad = dot_t(qkv_grad, qkv_weight)
    residual_grad, gain1_grad, shift1_grad = jax.vjp(layer_norm, residual, gain1, shift1)[1](normed_grad)
    residual_grad = residual_grad + hidden_grad
    grads = (gain1_grad, shift1_grad, qkv_weight_grad, qv_bias_grad, out_weight_grad, out_bias_grad,
             gain2_grad, shift2_grad, up_weight_grad, up_bias_grad, down_weight_grad, down_bias_grad)
    return residual_grad, grads


def band_sums(band_view):
    sums = jnp.stack([jnp.sum(band_view, axis=(0, 1, 3)), jnp.sum(band_view * band_view, axis=(0, 1, 3))])
    sums = sums + swap(sums, "core")
    sums = jnp.sum(gather_small(sums, "y"), axis=0)
    sums = jnp.sum(gather_small(sums, "x"), axis=0)
    return sums + swap(sums, "z_hi")


def per_device(
    pixels, visible_counts, visible_index, running_mean, running_var, patch_weight, patch_bias,
    enc_ln1_gain, enc_ln1_shift, enc_qkv_weight, enc_qv_bias, enc_out_weight, enc_out_bias,
    enc_ln2_gain, enc_ln2_shift, enc_up_weight, enc_up_bias, enc_down_weight, enc_down_bias,
    dec_embed_weight, dec_embed_bias, mask_token, dec_ln1_gain, dec_ln1_shift, dec_qkv_weight,
    dec_qv_bias, dec_out_weight, dec_out_bias, dec_ln2_gain, dec_ln2_shift, dec_up_weight,
    dec_up_bias, dec_down_weight, cotangent,
):
    pipe = lax.axis_index("z_lo")
    items, patches, half_pix = pixels.shape
    bands_here = running_mean.shape[0]
    band_pix = half_pix // bands_here
    width, dec_width = patch_weight.shape[1], dec_embed_weight.shape[1]

    enc_vector = jnp.concatenate([patch_bias, enc_ln1_gain, enc_ln1_shift, enc_out_bias, enc_ln2_gain,
                                  enc_ln2_shift, enc_down_bias, enc_qv_bias, enc_up_bias])
    dec_vector = jnp.concatenate([dec_embed_bias, mask_token, dec_ln1_gain, dec_ln1_shift, dec_out_bias,
                                  dec_ln2_gain, dec_ln2_shift, dec_qv_bias, dec_up_bias])
    vector = jnp.concatenate([jnp.pad(enc_vector, (0, 128 - enc_vector.shape[0])),
                              jnp.pad(dec_vector, (0, 128 - dec_vector.shape[0]))])[None, :]
    wide_e = (4 * width + dec_width) // 2
    wide_d = 2 * dec_width
    wide_up = enc_up_weight.shape[1] // 2
    (
        (enc_qkv, enc_out, embed, dec_qkv, dec_out),
        (enc_up, dec_up),
        (enc_down, dec_down, patch_full, vectors),
    ) = gather_weights(
        jnp.concatenate([enc_qkv_weight, enc_out_weight, dec_embed_weight], axis=1), enc_up_weight,
        enc_down_weight, jnp.concatenate([dec_qkv_weight, dec_out_weight], axis=1), dec_up_weight,
        dec_down_weight, patch_weight, vector,
    )
    patch_rows = lax.dynamic_slice_in_dim(patch_full, pipe * half_pix, half_pix, axis=0)
    devices = vectors.shape[0]

    def unpack(rows, unit):
        singles = rows[:, : 7 * unit].reshape(devices, 7, unit).transpose(1, 0, 2).reshape(7, -1)
        double = rows[:, 7 * unit : 9 * unit].reshape(-1)
        quad = rows[:, 9 * unit : 13 * unit].reshape(-1)
        return singles, double, quad

    enc_s, enc_qv, enc_upb = unpack(vectors[:, :128], 6)
    dec_s, dec_qv, dec_upb = unpack(vectors[:, 128:], 4)
    encoder = (enc_s[1], enc_s[2], enc_qkv, enc_qv, enc_out, enc_s[3], enc_s[4], enc_s[5], enc_up, enc_upb,
               enc_down, enc_s[6])
    decoder = (dec_s[2], dec_s[3], dec_qkv, dec_qv, dec_out, dec_s[4], dec_s[5], dec_s[6], dec_up, dec_upb,
               dec_down, jnp.zeros((dec_width,), F32))

    band_view = pixels.reshape(items, patches, bands_here, band_pix)
    band_total, band_square = band_sums(band_view)
    population = 64 * items * patches * band_pix
    band_mean = band_total / population
    band_var = band_square / population - band_mean * band_mean
    band_scale = lax.rsqrt(band_var + band_epsilon)
    band_means = 0.9 * running_mean + 0.1 * band_mean
    band_variances = 0.9 * running_var + 0.1 * band_var
    normalized = ((band_view - band_mean[:, None]) * band_scale[:, None]).reshape(items, patches, half_pix)

    index = jnp.pad(visible_index, ((0, 0), (0, SLOTS - visible_index.shape[1])))
    keep = jnp.arange(SLOTS)[None, :] < visible_counts[:, None]
    onehot = (
        (index[:, :, None] == jnp.arange(GRID)[None, None, :]) & keep[:, :, None]
    ).astype(BF16)
    picked = jnp.einsum("ivp,iph->ivh", onehot[:, :, :patches], normalized.astype(BF16),
                        preferred_element_type=F32).astype(BF16)
    embedded = jnp.einsum("ivh,hd->ivd", picked, patch_rows, preferred_element_type=F32).astype(BF16)
    other_half = swap(take(embedded, 1 - pipe), "z_lo")
    my_onehot = take(onehot, pipe)
    my_count = lax.dynamic_slice_in_dim(visible_counts, pipe, 1)
    start_rows = (
        take(embedded, pipe).astype(F32) + other_half.astype(F32) + enc_s[0] + position_rows(take(index, pipe), width)
    )
    hidden, active, enc_stored = block_forward(start_rows, encoder, HEADS, my_count)
    encoded = (hidden + (dot(active, enc_down) + encoder[11])).astype(BF16)
    latent = (dot(encoded, embed) + dec_s[0]).astype(BF16)
    covered = jnp.sum(my_onehot.astype(F32), axis=0)
    bare = jnp.where(jnp.arange(GRID) < patches, 1.0 - covered, 0.0)[:, None]
    grid = t_dot(my_onehot, latent) + bare * dec_s[1] + position_rows(jnp.arange(GRID), dec_width)
    grid_count = jnp.full((1,), patches, jnp.int32)
    _, _, dec_stored = block_forward(grid, decoder, DHEADS, grid_count)
    target = jnp.pad(take(cotangent, pipe), ((0, GRID - patches), (0, 0)))
    grid_grad, dec_grads = block_backward(target, dec_stored, decoder, DHEADS, grid_count)
    mask_grad = jnp.sum(bare * grid_grad, axis=0)
    latent_grad = dot(my_onehot, grid_grad.astype(BF16)).astype(BF16)
    embed_bias_grad = jnp.sum(latent_grad.astype(F32), axis=0)
    encoded_grad = dot_t(latent_grad, embed).astype(BF16).astype(F32)
    start_grad, enc_grads = block_backward(encoded_grad, enc_stored, encoder, HEADS, my_count)
    start_low = start_grad.astype(BF16)
    patch_bias_grad = jnp.sum(start_low.astype(F32), axis=0)
    both = jnp.where(pipe == 0, 1, 0)
    start_other = swap(start_low, "z_lo")
    start_pair = jnp.where(both, jnp.stack([start_low, start_other]), jnp.stack([start_other, start_low]))
    picked_grad = jnp.einsum("ivd,hd->ivh", start_pair, patch_rows, preferred_element_type=F32).astype(BF16)
    placed = jnp.einsum("ivp,ivh->iph", onehot[:, :, :patches], picked_grad, preferred_element_type=F32)
    pixel_grad = (
        placed.reshape(items, patches, bands_here, band_pix) * band_scale[:, None]
    ).reshape(items, patches, half_pix)

    def repack(singles, double, quad, unit):
        cut = jnp.stack(singles).reshape(7, devices, unit).transpose(1, 0, 2).reshape(devices, 7 * unit)
        rows = jnp.concatenate([cut, double.reshape(devices, -1), quad.reshape(devices, -1)], axis=1)
        return jnp.pad(rows, ((0, 0), (0, 128 - rows.shape[1])))

    (eg1, es1, eqkv, eqv, eout, eob, eg2, es2, eup, eub, edown, edb) = enc_grads
    (dg1, ds1, dqkv, dqv, dout, dob, dg2, ds2, dup, dub, ddown, _) = dec_grads
    vector_grads = jnp.concatenate([
        repack([patch_bias_grad, eg1, es1, eob, eg2, es2, edb], eqv, eub, 6),
        repack([embed_bias_grad, mask_grad, dg1, ds1, dob, dg2, ds2], dqv, dub, 4),
    ], axis=1)
    shape_a, shape_b = (2, 4, 2, 2, 480, 256), (2, 2, 2, 4, 416, 256)
    part_a = wide_grad(*dqkv, None, shape_a, "xz", 32, 0, 0, 4)
    part_a = wide_grad(*dout, part_a, shape_a, "xz", 32, 0, 6, 4)
    part_b = wide_grad(*dup, None, shape_b, "zx", 32, 9, 0, 4)
    pipe_id = pipe.astype(jnp.int32).reshape(1)
    part_c = tall_grad(*ddown, None, 32, 5, pipe_id, 2)
    part_a = wide_grad(encoded, latent_grad[None], part_a, shape_a, "xz", 48, 3, 12, 7)
    part_b = wide_grad(*eup, part_b, shape_b, "zx", 48, 0, 0, 6)
    part_c = tall_grad(*edown, part_c, 48, 0, pipe_id, 1)
    part_a = wide_grad(*eout, part_a, shape_a, "xz", 48, 3, 9, 7)
    part_a = wide_grad(*eqkv, part_a, shape_a, "xz", 48, 3, 0, 7)
    part_c = tall_grad(
        picked.reshape(-1, half_pix), start_pair.reshape(-1, width), part_c, 24, 3, pipe_id, 1)
    cut = vector_grads.astype(BF16).reshape(2, 4, 2, 4, 2, 2, 1, 128)
    cut = jnp.pad(cut.transpose(5, 3, 0, 2, 1, 4, 6, 7), ((0, 0),) * 6 + ((0, 3), (0, 0)))
    part_c = lax.dynamic_update_slice(part_c, cut.reshape(2, 4, 2, 2, 4, 8, 128), (0, 0, 0, 0, 0, 312, 0))
    out6, out_up, out_down, out4, out_dup, out_ddown, out_patch, out_vector = scatter_grads(
        part_a, part_b, part_c, wide_e, wide_up, wide_d)
    ev, dv = out_vector[:128], out_vector[128:]
    return (
        band_means, band_variances, pixel_grad, out_patch, ev[:6], ev[6:12], ev[12:18],
        out6[:, : 3 * width], ev[42:54], out6[:, 3 * width : 4 * width], ev[18:24], ev[24:30], ev[30:36],
        out_up, ev[54:78], out_down, ev[36:42], out6[:, 4 * width :], dv[:4], dv[4:8], dv[8:12], dv[12:16],
        out4[:, : 3 * dec_width], dv[28:36], out4[:, 3 * dec_width :], dv[16:20], dv[20:24], dv[24:28],
        out_dup, dv[36:52], out_ddown,
    )


def solution(mesh):
    whole = P(ALL)
    sizes = (2, 4, 2, 4, 2)
    cube = Mesh(mesh.devices.reshape(sizes), ALL)
    placed = (P(DP, None, "z_lo"), P(DP), P(DP, None), P("z_lo"), P("z_lo")) + (whole,) * 28 + (P(DP, None, None),)
    return jax.shard_map(
        per_device,
        mesh=cube,
        in_specs=placed,
        out_specs=(P("z_lo"), P("z_lo"), P(DP, None, "z_lo")) + (whole,) * 28,
        check_vma=False,
    )
```

```python
import functools
import math

import jax
import jax.numpy as jnp
from jax import lax
from jax.experimental import pallas as pl
from jax.experimental.pallas import tpu as pltpu
from jax.sharding import Mesh
from jax.sharding import PartitionSpec as P

HEADS = 12
DHEADS = 16
SLOTS = 256
GRID = 592

band_epsilon = 1e-05
norm_epsilon = 1e-06
masked_score = -1e30

PIPE = ("z_lo",)
DP = ("x", "z_hi", "y", "core")
ALL = PIPE + DP
RING = {"x": ("x",), "y": ("y",), "z": ("z_lo", "z_hi")}
F32 = jnp.float32
BF16 = jnp.bfloat16


def along(axis, place):
    return (place % 2) * 2 + place // 2 if axis == "z" else place


def ring_place(axis):
    if axis == "z":
        return lax.axis_index("z_hi") * 2 + lax.axis_index("z_lo")
    return lax.axis_index(axis)


def shift(value, axis, step, mirrored):
    pairs = []
    for place in range(4):
        for core in range(2):
            target = (place + (-step if mirrored and core else step)) % 4
            pairs.append((along(axis, place) * 2 + core, along(axis, target) * 2 + core))
    return lax.ppermute(value, RING[axis] + ("core",), pairs)


def swap(value, axis):
    return lax.ppermute(value, axis, [(0, 1), (1, 0)])


def put(blocks, block, index):
    return lax.dynamic_update_slice_in_dim(blocks, block[None], index, axis=0)


def take(blocks, index):
    return lax.dynamic_index_in_dim(blocks, index, axis=0, keepdims=False)


def direction():
    return jnp.where(lax.axis_index("core") == 0, 1, 3)


def by_core(mine, other):
    first = lax.axis_index("core") == 0
    return jnp.where(first, mine, other), jnp.where(first, other, mine)


def halves(array):
    rows, columns = array.shape
    return array.reshape(rows, 2, columns // 2).transpose(1, 0, 2)


def chunks(array, width):
    *lead, rows, columns = array.shape
    count = columns // width
    cut = jnp.moveaxis(array.reshape(*lead, rows, count, width), -2, -3)
    return cut.reshape(*lead, count * rows, width)


def pad_rows(array, rows):
    return jnp.pad(array, ((0, rows - array.shape[0]), (0, 0)))


def share(block, axes):
    count = lax.axis_size(axes)
    spread = jnp.broadcast_to(block[None], (count,) + block.shape)
    return lax.all_to_all(spread, axes, 0, 0)


def ring_share(block, axis):
    back = [shift(block, axis, step, False) for step in (3, 2, 1)] + [block]
    return lax.dynamic_slice_in_dim(jnp.stack(back + back[:3]), 3 - ring_place(axis), 4)


def sum_shares(blocks, axes):
    return jnp.sum(lax.all_to_all(blocks, axes, 0, 0).astype(F32), axis=0)


def after(value, *earlier):
    return lax.optimization_barrier((value,) + earlier)[0]


def join_kernel(*refs):
    ins, out = refs[:-1], refs[-1]
    for side in range(2):
        rows = [r[...].astype(F32).reshape(1, -1) for r in ins[side * 9 : side * 9 + 9]]
        rows.append(jnp.zeros((1, 128 - sum(r.shape[1] for r in rows)), F32))
        out[:, side * 128 : side * 128 + 128] = jnp.concatenate(rows, axis=1).astype(BF16)


def join(vectors):
    return pl.pallas_call(join_kernel, out_shape=jax.ShapeDtypeStruct((1, 256), BF16))(*vectors)


def core_id():
    return lax.axis_index("core").astype(jnp.int32).reshape(1)


def direct_sum(blocks, axis):
    me = ring_place(axis)
    total = take(blocks, me).astype(F32)
    for step in (1, 2, 3):
        total = total + shift(take(blocks, (me + step) % 4), axis, step, False).astype(F32)
    return total.astype(BF16)


def together(*values):
    return lax.optimization_barrier(values)


def held_kernel(value, *rest):
    pass


def hold(value, *earlier):
    anywhere = pl.BlockSpec(memory_space=pl.ANY)
    return pl.pallas_call(
        held_kernel,
        out_shape=jax.ShapeDtypeStruct(value.shape, value.dtype),
        in_specs=[anywhere] * (1 + len(earlier)),
        out_specs=anywhere,
        input_output_aliases={0: 0},
    )(value, *earlier)


def on_each_core(core_ref, mine, other, work):
    @pl.when(core_ref[0] == 0)
    def _():
        work((mine, other))

    @pl.when(core_ref[0] != 0)
    def _():
        work((other, mine))


def pack_enc_kernel(raw, out):
    def rows_of(first, last, rows):
        return [raw[y, c, :, first:last].astype(F32)[:rows] for y in range(4) for c in range(2)]

    for j in range(13):
        at = j * 48
        out[at : at + 48, :] = jnp.concatenate(rows_of(j * 256, j * 256 + 256, 6), axis=0).astype(BF16)
    parts = []
    for y in range(4):
        for c in range(2):
            for g in range(3):
                parts.append(raw[y, c, :, 3328 + g * 384 : 3712 + g * 384].astype(F32))
    down = jnp.concatenate(parts, axis=0).astype(BF16)
    out[624:816, :] = down[:, :256]
    out[816:912, :128] = down[:96, 256:]
    out[816:912, 128:] = down[96:, 256:]


def pack_enc(raw):
    return pl.pallas_call(
        pack_enc_kernel,
        out_shape=jax.ShapeDtypeStruct((912, 256), BF16),
        compiler_params=pltpu.CompilerParams(vmem_limit_bytes=24 << 20),
    )(raw)


def unpack_call(kernel, part, block, index, outs):
    return pl.pallas_call(
        kernel,
        out_shape=[jax.ShapeDtypeStruct(o, BF16) for o in outs],
        grid_spec=pltpu.PrefetchScalarGridSpec(
            num_scalar_prefetch=1,
            grid=(2, 4),
            in_specs=[pl.BlockSpec(block, index)] * 2,
            out_specs=[pl.BlockSpec((o[0] // 8, o[1]), lambda zl, x, c: (zl * 4 + x, 0)) for o in outs],
        ),
        compiler_params=pltpu.CompilerParams(vmem_limit_bytes=40 << 20),
    )(core_id(), part, swap(part, "core"))


def unpack_enc_kernel(core_ref, mine, other, qkv, out, embed, up, down):
    def work(sides):
        for zh in range(2):
            rows = slice(zh * 48, zh * 48 + 48)
            for j in range(14):
                at = j % 7 * 48
                value = sides[j // 7][0, zh, 0, at : at + 48, :]
                target, k = (qkv, j) if j < 9 else (out, j - 9) if j < 12 else (embed, j - 12)
                target[rows, k * 256 : k * 256 + 256] = value
            for j in range(12):
                at = 336 + j % 6 * 48
                up[rows, j * 256 : j * 256 + 256] = sides[j // 6][0, zh, 0, at : at + 48, :]
            for side in range(2):
                ref, at, k = sides[side], side * 384, zh * 192
                down[k : k + 192, at : at + 256] = ref[0, zh, 0, 624:816, :]
                down[k : k + 96, at + 256 : at + 384] = ref[0, zh, 0, 816:912, :128]
                down[k + 96 : k + 192, at + 256 : at + 384] = ref[0, zh, 0, 816:912, 128:]

    on_each_core(core_ref, mine, other, work)


def unpack_enc(part):
    outs = [(768, 2304), (768, 768), (768, 512), (768, 3072), (3072, 768)]
    return unpack_call(
        unpack_enc_kernel, part, (1, 2, 1, 912, 256), lambda zl, x, c: (x, 0, zl, 0, 0), outs)


def unpack_dec_kernel(place_ref, *refs):
    blocks, (qkv, out, up, down, wide) = (refs[:4], refs[4:8]), refs[8:]
    for which in range(2):
        side = place_ref[0] if which == 0 else 1 - place_ref[0]
        for step in range(4):
            y = lax.rem(place_ref[1] + jnp.where(side == 0, 4 - step, step), 4)
            for zh in range(2):
                ref, k = blocks[which][step], zh * 4 + y
                values = ref[0, zh, 0, 0:64, :].astype(F32)
                for j in range(8):
                    wide[pl.ds(pl.multiple_of(k * 8, 8), 8), j * 256 : j * 256 + 256] = values[j * 8 : j * 8 + 8]
                down[
                    pl.ds(pl.multiple_of(k * 32, 32), 32), pl.ds(pl.multiple_of(side * 256, 256), 256)
                ] = ref[0, zh, 0, 64:96, :]

        def store(number):
            whole = wide[...].astype(BF16)
            if number == 0:
                qkv[:, :1024] = whole[:, :1024]
            else:
                qkv[:, 1024:] = whole[:, :512]
                out[...] = whole[:, 512:1024]
            up[:, number * 1024 : number * 1024 + 1024] = whole[:, 1024:]

        pl.when(side == 0)(functools.partial(store, 0))
        pl.when(side == 1)(functools.partial(store, 1))


def unpack_dec(mine, other):
    outs = [(512, 1536), (512, 512), (512, 2048), (2048, 512)]
    place = jnp.stack([lax.axis_index("core"), ring_place("y")]).astype(jnp.int32)
    return pl.pallas_call(
        unpack_dec_kernel,
        out_shape=[jax.ShapeDtypeStruct(o, BF16) for o in outs],
        grid_spec=pltpu.PrefetchScalarGridSpec(
            num_scalar_prefetch=1,
            grid=(2, 4),
            in_specs=[pl.BlockSpec((1, 2, 1, 96, 256), lambda zl, x, c: (x, 0, zl, 0, 0))] * 8,
            out_specs=[pl.BlockSpec((o[0] // 8, o[1]), lambda zl, x, c: (zl * 4 + x, 0)) for o in outs],
            scratch_shapes=[pltpu.VMEM((64, 2048), F32)],
        ),
        compiler_params=pltpu.CompilerParams(vmem_limit_bytes=40 << 20),
    )(place, *mine, *other)


def cut(array):
    both = halves(array)
    core = lax.axis_index("core")
    return take(both, core), take(both, 1 - core)


def gather_enc(enc6, enc_up, enc_down, vector):
    def enc(which):
        rows = [pad_rows(p, 8) for p in (cut(enc6)[which], cut(enc_up)[which])]
        tall = cut(enc_down)[which].reshape(3, 8, -1).transpose(1, 0, 2).reshape(8, -1)
        return jnp.concatenate(rows + [tall, pad_rows(cut(vector)[which], 8)], axis=1)

    raw = jnp.stack(by_core(enc(0), swap(enc(1), "core")))
    raw = ring_share(raw, "y")
    part = lax.all_gather(pack_enc(raw), ("x", "z_hi", "z_lo"), tiled=False).reshape(4, 2, 2, 912, 256)
    return part, raw[:, :, 0, 4480:].reshape(8, 128)


def gather_patch(patch, stats):
    mine, other = cut(patch)
    rows = jnp.concatenate(by_core(mine, swap(other, "core")), axis=0)
    flat = stats.reshape(1, -1)
    high = lax.reduce_precision(flat, 8, 7)
    mid = lax.reduce_precision(flat - high, 8, 7)
    three = jnp.concatenate([high, mid, flat - high - mid], axis=0)
    three = jnp.pad(three, ((0, 5), (0, rows.shape[1] - three.shape[1]))).astype(BF16)
    blocks = share(jnp.concatenate([rows, three], axis=0), ("x", "z_hi", "y"))
    stats = jnp.sum(blocks[:, 24:27, : flat.shape[1]].astype(F32), axis=(0, 1)).reshape(stats.shape)
    rows = blocks[:, :24].reshape(-1, rows.shape[1])
    return jnp.concatenate(by_core(rows, swap(rows, "core")), axis=1), stats


def gather_dec(dec4, dec_up, dec_down, vectors, started):
    def dec(which):
        wide = jnp.concatenate([cut(dec4)[which], cut(dec_up)[which]], axis=1)
        return wide, cut(dec_down)[which]

    mine, other = dec(0), dec(1)
    wide = jnp.concatenate(by_core(mine[0], swap(other[0], "core")), axis=0)
    tall = jnp.concatenate(by_core(mine[1], swap(other[1], "core")), axis=0)
    vectors = jnp.pad(vectors, ((0, 0), (0, 128)))
    part = after(jnp.concatenate([chunks(wide, 256), tall, vectors], axis=0), started)
    part = share(part, ("x", "z_hi", "z_lo"))
    vectors = part[:, 96:, :128].reshape(128, 128)
    low, high = by_core(vectors, swap(vectors, "core"))
    return part[:, :96].reshape(4, 2, 2, 96, 256), jnp.concatenate([low, high], axis=1)


def spread_kernel(vectors, *outs):
    values = vectors[...]
    for side, unit in ((0, 6), (1, 4)):
        for k, (times, first, count) in enumerate(((1, 0, 7), (2, 7, 1), (4, 9, 1))):
            size = unit * times
            length = size * 128
            place = lax.broadcasted_iota(jnp.int32, (128, length), 1)
            row = lax.broadcasted_iota(jnp.int32, (128, length), 0)
            device = (row & 8) * 8 + (row >> 5) * 16 + (row & 16) // 2 + (row & 7)
            lifted = (place >= device * size) & (place < device * size + size)
            table = lax.dot_general(
                values[:, side * 128 : side * 128 + 128], lifted.astype(BF16),
                (((0,), (0,)), ((), ())), preferred_element_type=F32)
            inside = place[:1] - lax.div(place[:1], size) * size
            for n in range(count):
                wanted = row == inside + (first + n) * unit
                outs[side * 3 + k][n : n + 1, :] = jnp.sum(jnp.where(wanted, table, 0.0), axis=0, keepdims=True)


def spread(vectors):
    shapes = [(8, 768), (1, 1536), (1, 3072), (8, 512), (1, 1024), (1, 2048)]
    return pl.pallas_call(
        spread_kernel,
        out_shape=[jax.ShapeDtypeStruct(s, F32) for s in shapes],
        compiler_params=pltpu.CompilerParams(vmem_limit_bytes=24 << 20),
    )(vectors)


def collect_kernel(*refs):
    ins, out = refs[:-1], refs[-1]
    for side, unit in ((0, 6), (1, 4)):
        total = jnp.zeros((128, 128), F32)
        for k, (times, first, count) in enumerate(((1, 0, 7), (2, 7, 1), (4, 9, 1))):
            size = unit * times
            length = size * 128
            place = lax.broadcasted_iota(jnp.int32, (128, length), 1)
            row = lax.broadcasted_iota(jnp.int32, (128, length), 0)
            lifted = (place >= row * size) & (place < row * size + size)
            inside = place[:1] - lax.div(place[:1], size) * size
            table = jnp.zeros((128, length), F32)
            for n in range(count):
                given = ins[side * 9 + n + (0, 7, 8)[k]][...].reshape(1, -1)
                table = jnp.where(row == inside + (first + n) * unit, given, table)
            total = total + lax.dot_general(
                lifted.astype(BF16), table.astype(BF16), (((1,), (1,)), ((), ())), preferred_element_type=F32)
        out[:, side * 128 : side * 128 + 128] = total.astype(BF16)


def collect(*vectors):
    return pl.pallas_call(
        collect_kernel,
        out_shape=jax.ShapeDtypeStruct((128, 256), BF16),
        compiler_params=pltpu.CompilerParams(vmem_limit_bytes=24 << 20),
    )(*vectors)


def wide_grad_kernel(order, rows, lhs, rhs, *rest):
    out, turned = rest[-2:]

    @pl.when(pl.program_id(0) == 0)
    def _():
        turned[...] = lhs[...].T

    result = jnp.dot(turned[...], rhs[0], preferred_element_type=F32).astype(BF16)
    for block in range(16):
        zl, x, zh = block // 8, block // 2 % 4, block % 2
        spot = (0, x, zh, zl) if order == "xz" else (0, zh, zl, x)
        out[spot] = result[block * rows : block * rows + rows]


def wide_grad(lhs, rhs, buffer, shape, order, rows, row_block, first, per_side):
    length, height = lhs.shape
    parts, _, width = rhs.shape
    per_part = width // 256
    block = (1, 4, 2, 2, rows, 256) if order == "xz" else (1, 2, 2, 4, rows, 256)

    def place(j):
        chunk = j + first
        return (chunk // per_side, 0, 0, 0, row_block + chunk % per_side, 0)

    given = () if buffer is None else (buffer,)
    return pl.pallas_call(
        functools.partial(wide_grad_kernel, order, rows),
        out_shape=jax.ShapeDtypeStruct(shape, BF16),
        grid=(parts * per_part,),
        in_specs=[
            pl.BlockSpec((length, height), lambda j: (0, 0)),
            pl.BlockSpec((1, length, 256), lambda j: (j // per_part, 0, j % per_part)),
        ] + [pl.BlockSpec(memory_space=pl.ANY)] * len(given),
        out_specs=pl.BlockSpec(block, place),
        scratch_shapes=[pltpu.VMEM((height, length), BF16)],
        input_output_aliases={2: 0} if given else {},
        compiler_params=pltpu.CompilerParams(vmem_limit_bytes=40 << 20),
        cost_estimate=pl.CostEstimate(
            flops=2 * length * height * width * parts, transcendentals=0,
            bytes_accessed=2 * (length * height + parts * length * width + parts * height * width)),
    )(lhs, rhs, *given)


def tall_grad_kernel(lhs, rhs, out, turned):
    @pl.when(pl.program_id(0) == 0)
    def _():
        turned[...] = lhs[...].T

    result = jnp.dot(turned[...], rhs[...], preferred_element_type=F32).astype(BF16)
    for block in range(16):
        zl, x, zh = block // 8, block // 2 % 4, block % 2
        out[0, x, zh, zl, :, :128] = result[block * 192 : block * 192 + 96]
        out[0, x, zh, zl, :, 128:] = result[block * 192 + 96 : block * 192 + 192]


def tall_grad(lhs, rhs, shape):
    length, height = lhs.shape
    return pl.pallas_call(
        tall_grad_kernel,
        out_shape=jax.ShapeDtypeStruct(shape, BF16),
        grid=(6,),
        in_specs=[pl.BlockSpec((length, height), lambda j: (0, 0)), pl.BlockSpec((length, 128), lambda j: (0, j))],
        out_specs=pl.BlockSpec((1, 4, 2, 2, 96, 256), lambda j: (j // 3, 0, 0, 0, j % 3, 0)),
        scratch_shapes=[pltpu.VMEM((height, length), BF16)],
        compiler_params=pltpu.CompilerParams(vmem_limit_bytes=40 << 20),
        cost_estimate=pl.CostEstimate(
            flops=2 * length * height * rhs.shape[1], transcendentals=0, bytes_accessed=4 * height * rhs.shape[1]),
    )(lhs, rhs)


def add_cores_kernel(info, *refs):
    out = refs[-1]
    at = 0
    for mine, got in zip(refs[0:4:2], refs[1:4:2], strict=True):
        rows = got.shape[1]
        out[0, at : at + rows, :] = (mine[0, 0].astype(F32) + got[0].astype(F32)).astype(BF16)
        at += rows


def add_cores(first, second, *earlier):
    core = lax.axis_index("core")
    operands, specs, rows = [], [], 0
    for part, got in (first, second):
        count = part.shape[-2]
        operands += [part.reshape(2, 16, count, 256), got.reshape(16, count, 256)]
        specs += [
            pl.BlockSpec((1, 1, count, 256), lambda i, info: (info[0], i, 0, 0)),
            pl.BlockSpec((1, count, 256), lambda i, info: (i, 0, 0))]
        rows += count
    return pl.pallas_call(
        add_cores_kernel,
        out_shape=jax.ShapeDtypeStruct((16, rows, 256), BF16),
        grid_spec=pltpu.PrefetchScalarGridSpec(
            num_scalar_prefetch=1,
            grid=(16,),
            in_specs=specs + [pl.BlockSpec(memory_space=pl.ANY)] * len(earlier),
            out_specs=pl.BlockSpec((1, rows, 256), lambda i, info: (i, 0, 0)),
        ),
        compiler_params=pltpu.CompilerParams(vmem_limit_bytes=24 << 20),
    )(core.astype(jnp.int32).reshape(1), *operands, *earlier)


def core_got(part):
    return part, swap(take(part, 1 - lax.axis_index("core")), "core")


def core_sum(part):
    core = lax.axis_index("core")
    got = swap(take(part, 1 - core), "core")
    return (take(part, core).astype(F32) + got.astype(F32)).astype(BF16)


def finish(mine, other):
    return by_core(mine, swap(other, "core"))


def finish_pair(pair):
    core = lax.axis_index("core")
    return finish(take(pair, core), take(pair, 1 - core))


def join_columns(sides, first, last, rows):
    return jnp.concatenate([side[:rows, first:last] for side in sides], axis=1).astype(F32)


def by_row_kernel(arrived, rest, out):
    last = jnp.zeros((336, 256), F32)
    for block in range(16):
        last = last + arrived[block].astype(F32)
    rest = rest[...].astype(F32)
    out[...] = jnp.zeros_like(out)

    def chunk(value, at, rows):
        for k in range(8):
            out[k // 2, k % 2, 0:rows, at : at + 256] = value[k * rows : (k + 1) * rows].astype(BF16)

    for j in range(7):
        chunk(last[j * 48 : j * 48 + 48], j * 256, 6)
    for j in range(6):
        chunk(rest[672 + j * 48 : 720 + j * 48], 1792 + j * 256, 6)
    for j in range(8):
        chunk(rest[j * 32 : j * 32 + 32], 4480 + j * 256, 4)
    for k in range(8):
        y, c = k // 2, k % 2
        for g in range(3):
            for j in range(3):
                n = k % 4 * 24 + g * 8
                value = rest[384 + j * 96 + n : 392 + j * 96 + n, k // 4 * 128 : k // 4 * 128 + 128]
                at = 3328 + g * 384 + j * 128
                out[y, c, :, at : at + 128] = value.astype(BF16)
        for g in range(2):
            n = 256 + k * 16 + g * 8
            out[y, c, :, 6528 + g * 256 : 6784 + g * 256] = rest[n : n + 8].astype(BF16)


def by_row(arrived, rest):
    return pl.pallas_call(
        by_row_kernel,
        out_shape=jax.ShapeDtypeStruct((4, 2, 8, 7040), BF16),
        compiler_params=pltpu.CompilerParams(vmem_limit_bytes=40 << 20),
    )(arrived, rest)


def outputs_kernel(low, high, enc6, up, down, dec4, dup, ddown):
    for side, ref in ((0, low), (1, high)):
        value = ref[...].astype(F32)
        enc6[:, side * 1792 : side * 1792 + 1792] = value[:6, :1792]
        up[:, side * 1536 : side * 1536 + 1536] = value[:6, 1792:3328]
        for g in range(3):
            down[g * 8 : g * 8 + 8, side * 384 : side * 384 + 384] = value[:, 3328 + g * 384 : 3712 + g * 384]
        dec4[:, side * 1024 : side * 1024 + 1024] = value[:4, 4480:5504]
        dup[:, side * 1024 : side * 1024 + 1024] = value[:4, 5504:6528]
        for g in range(2):
            ddown[g * 8 : g * 8 + 8, side * 256 : side * 256 + 256] = value[:, 6528 + g * 256 : 6784 + g * 256]


def outputs(low, high):
    shapes = [(6, 3584), (6, 3072), (24, 768), (4, 2048), (4, 2048), (16, 512)]
    return pl.pallas_call(
        outputs_kernel,
        out_shape=[jax.ShapeDtypeStruct(s, F32) for s in shapes],
        compiler_params=pltpu.CompilerParams(vmem_limit_bytes=24 << 20),
    )(low, high)


def sum_over_y(blocks):
    core = lax.axis_index("core")
    pair = sum_shares(blocks, "y").astype(BF16)
    return outputs(*finish(take(pair, core), take(pair, 1 - core)))


def sum_patch(rows, vectors, earlier):
    pipe = lax.axis_index("z_lo")
    got = swap(take(vectors, 1 - pipe), "z_lo")
    vectors = (take(vectors, pipe).astype(F32) + got.astype(F32)).astype(BF16)
    vectors = vectors.transpose(4, 2, 1, 0, 3, 5)[..., None, :]
    vectors = jnp.pad(vectors, ((0, 0),) * 5 + ((0, 3), (0, 256)))
    rows = rows.astype(BF16).reshape(4, 2, 4, 2, 12, 2, 384).transpose(5, 2, 1, 0, 3, 4, 6)
    part = core_sum(jnp.concatenate([rows, vectors], axis=5))
    part = direct_sum(part, "y")
    zh = lax.axis_index("z_hi")
    got = swap(take(part, 1 - zh), "z_hi")
    part = (take(part, zh).astype(F32) + got.astype(F32)).astype(BF16)
    low, high = finish_pair(direct_sum(hold(part, earlier), "x"))
    return join_columns((low, high), 0, 384, 12), low[12, :128].astype(F32), high[12, :128].astype(F32)


def layer_norm(residual, gain, shift_row):
    center = residual - jnp.mean(residual, axis=-1, keepdims=True)
    spread = jnp.mean(center * center, axis=-1, keepdims=True)
    return center * lax.rsqrt(spread + norm_epsilon) * gain + shift_row


def frequencies(model_width):
    half_width = model_width // 2
    return jnp.exp(jnp.arange(half_width).astype(F32) * (-math.log(10000.0) / half_width))


def position_rows(places, model_width):
    phase_angle = places.astype(F32)[:, None] * frequencies(model_width)[None, :]
    return jnp.concatenate([jnp.sin(phase_angle), jnp.cos(phase_angle)], axis=1)


def dot(left, right):
    return jnp.dot(left, right, preferred_element_type=F32)


def dot_t(left, right):
    return lax.dot_general(left, right, (((1,), (1,)), ((), ())), preferred_element_type=F32)


def t_dot(left, right):
    return lax.dot_general(left, right, (((0,), (0,)), ((), ())), preferred_element_type=F32)


def attend_kernel(size, count_ref, q_ref, k_ref, v_ref, o_ref):
    length = q_ref.shape[0]
    q, k, v = q_ref[...], k_ref[...], v_ref[...]
    kept = lax.broadcasted_iota(jnp.int32, (1, length), 1) < count_ref[0]
    lane = lax.broadcasted_iota(jnp.int32, (1, 128), 1)
    total = jnp.zeros((length, 128), F32)
    for head in range(128 // size):
        mine = (lane >= head * size) & (lane < (head + 1) * size)
        scores = dot_t(jnp.where(mine, q, jnp.zeros_like(q)), k)
        scores = jnp.where(kept, scores * size ** (-0.5), masked_score)
        weight = jnp.exp(scores - jnp.max(scores, axis=1, keepdims=True))
        prob = (weight * (1.0 / jnp.sum(weight, axis=1, keepdims=True))).astype(BF16)
        total = total + dot(prob, jnp.where(mine, v, jnp.zeros_like(v)))
    o_ref[...] = total.astype(BF16)

def attend(qkv, heads, count):
    length, width = qkv.shape[0], qkv.shape[1] // 3
    groups = width // 128
    spec = lambda part: pl.BlockSpec((length, 128), lambda g, c, part=part: (0, part * groups + g))
    return pl.pallas_call(
        functools.partial(attend_kernel, width // heads),
        out_shape=jax.ShapeDtypeStruct((length, width), BF16),
        grid_spec=pltpu.PrefetchScalarGridSpec(
            num_scalar_prefetch=1, grid=(groups,),
            in_specs=[spec(0), spec(1), spec(2)],
            out_specs=pl.BlockSpec((length, 128), lambda g, c: (0, g))),
        compiler_params=pltpu.CompilerParams(vmem_limit_bytes=48 << 20),
    )(count, qkv, qkv, qkv)

def attend_back_kernel(size, count_ref, q_ref, k_ref, v_ref, g_ref, o_ref):
    length = q_ref.shape[0]
    q, k, v, g = q_ref[...], k_ref[...], v_ref[...], g_ref[...]
    kept = lax.broadcasted_iota(jnp.int32, (length, 1), 0) < count_ref[0]
    lane = lax.broadcasted_iota(jnp.int32, (1, 128), 1)
    dq = jnp.zeros((length, 128), F32)
    dk = jnp.zeros((length, 128), F32)
    dv = jnp.zeros((length, 128), F32)
    zero = jnp.zeros_like(q)
    for head in range(128 // size):
        mine = (lane >= head * size) & (lane < (head + 1) * size)
        q_h, k_h, g_h = jnp.where(mine, q, zero), jnp.where(mine, k, zero), jnp.where(mine, g, zero)
        scores = dot_t(k, q_h)
        scores = jnp.where(kept, scores * size ** (-0.5), masked_score)
        weight = jnp.exp(scores - jnp.max(scores, axis=0, keepdims=True))
        prob = weight * (1.0 / jnp.sum(weight, axis=0, keepdims=True))
        dv = dv + dot(prob.astype(BF16), g_h)
        prob_grad = dot_t(v, g_h)
        inner = jnp.sum(prob * prob_grad, axis=0, keepdims=True)
        score_grad = (prob * (prob_grad - inner)).astype(BF16)
        dk = dk + dot(score_grad, q_h)
        dq = dq + t_dot(score_grad, k_h)
    o_ref[0] = (dq * size ** (-0.5)).astype(BF16)
    o_ref[1] = (dk * size ** (-0.5)).astype(BF16)
    o_ref[2] = dv.astype(BF16)

def attend_back(qkv, grad, heads, count):
    length, width = qkv.shape[0], qkv.shape[1] // 3
    groups = width // 128
    spec = lambda part: pl.BlockSpec((length, 128), lambda g, c, part=part: (0, part * groups + g))
    return pl.pallas_call(
        functools.partial(attend_back_kernel, width // heads),
        out_shape=jax.ShapeDtypeStruct((3, length, width), BF16),
        grid_spec=pltpu.PrefetchScalarGridSpec(
            num_scalar_prefetch=1, grid=(groups,),
            in_specs=[spec(0), spec(1), spec(2), spec(0)],
            out_specs=pl.BlockSpec((3, length, 128), lambda g, c: (0, 0, g))),
        compiler_params=pltpu.CompilerParams(vmem_limit_bytes=56 << 20),
    )(count, qkv, qkv, qkv, grad)


def block_forward(residual, weights, head_count, key_keep):
    (gain1, shift1, qkv_weight, qv_bias, out_weight, out_bias, gain2, shift2, up_weight, up_bias,
     down_weight, down_bias) = weights
    width = residual.shape[1]
    normed = layer_norm(residual, gain1, shift1).astype(BF16)
    qkv_bias = jnp.concatenate([qv_bias[:width], jnp.zeros((width,), F32), qv_bias[width:]])
    qkv_rows = (dot(normed, qkv_weight) + qkv_bias).astype(BF16)
    attended = attend(qkv_rows, head_count, key_keep)
    hidden = residual + (dot(attended, out_weight) + out_bias)
    second = layer_norm(hidden, gain2, shift2).astype(BF16)
    up_proj = dot(second, up_weight) + up_bias
    active = jax.nn.gelu(up_proj).astype(BF16)
    stored = (residual, normed, qkv_rows, attended, hidden, second, up_proj, active)
    return hidden, active, stored


def block_backward(grad_out, stored, weights, head_count, key_keep, send):
    (gain1, shift1, qkv_weight, qv_bias, out_weight, out_bias, gain2, shift2, up_weight, up_bias,
     down_weight, down_bias) = weights
    (residual, normed, qkv_rows, attended, hidden, second, up_proj, active) = stored
    width = residual.shape[1]
    down_branch = grad_out.astype(BF16)
    down_bias_grad = jnp.sum(down_branch.astype(F32), axis=0)
    down_branch = send("down", active, down_branch)
    active_grad = dot_t(down_branch, down_weight)
    up_grad = send("gelu", None, jax.vjp(jax.nn.gelu, up_proj)[1](active_grad)[0].astype(BF16))
    up_bias_grad = jnp.sum(up_grad.astype(F32), axis=0)
    up_grad = send("up", second, up_grad)
    second_grad = dot_t(up_grad, up_weight)
    hidden_grad, gain2_grad, shift2_grad = jax.vjp(layer_norm, hidden, gain2, shift2)[1](second_grad)
    hidden_grad = hidden_grad + grad_out
    attn_branch = hidden_grad.astype(BF16)
    out_bias_grad = jnp.sum(attn_branch.astype(F32), axis=0)
    attn_branch = send("out", attended, attn_branch)
    attended_grad = send("attended", None, dot_t(attn_branch, out_weight).astype(BF16))
    qkv_parts = attend_back(qkv_rows, attended_grad, head_count, key_keep)
    qkv_parts = send("qkv", normed, qkv_parts)
    qkv_grad = jnp.concatenate([qkv_parts[0], qkv_parts[1], qkv_parts[2]], axis=1)
    qkv_sums = jnp.sum(qkv_grad.astype(F32), axis=0)
    qv_bias_grad = jnp.concatenate([qkv_sums[:width], qkv_sums[2 * width :]])
    normed_grad = dot_t(qkv_grad, qkv_weight)
    residual_grad, gain1_grad, shift1_grad = jax.vjp(layer_norm, residual, gain1, shift1)[1](normed_grad)
    residual_grad = residual_grad + hidden_grad
    vectors = (gain1_grad, shift1_grad, out_bias_grad, gain2_grad, shift2_grad, down_bias_grad)
    return residual_grad, vectors, qv_bias_grad, up_bias_grad


def band_sums(pixels, bands):
    items, patches, width = pixels.shape
    view = pixels.reshape(items, patches, bands, width // bands)
    sums = jnp.stack([jnp.sum(view, axis=(0, 1, 3)), jnp.sum(view * view, axis=(0, 1, 3))])
    return sums + swap(sums, "core")


def pixel_kernel(onehot, grad, scale, out):
    placed = lax.dot_general(
        onehot[0], grad[0], (((0,), (0,)), ((), ())), preferred_element_type=F32)
    out[0] = placed[: out.shape[1]] * scale[...]


def place_pixels(onehot, grad, scale, patches):
    items, slots, grid = onehot.shape
    width = grad.shape[2]
    return pl.pallas_call(
        pixel_kernel,
        out_shape=jax.ShapeDtypeStruct((items, patches, width), F32),
        grid=(items,),
        in_specs=[
            pl.BlockSpec((1, slots, grid), lambda i: (i, 0, 0)),
            pl.BlockSpec((1, slots, width), lambda i: (i, 0, 0)),
            pl.BlockSpec((1, width), lambda i: (0, 0)),
        ],
        out_specs=pl.BlockSpec((1, patches, width), lambda i: (i, 0, 0)),
        compiler_params=pltpu.CompilerParams(vmem_limit_bytes=24 << 20),
    )(onehot, grad, scale)


def per_device(
    pixels, visible_counts, visible_index, running_mean, running_var, patch_weight, patch_bias,
    enc_ln1_gain, enc_ln1_shift, enc_qkv_weight, enc_qv_bias, enc_out_weight, enc_out_bias,
    enc_ln2_gain, enc_ln2_shift, enc_up_weight, enc_up_bias, enc_down_weight, enc_down_bias,
    dec_embed_weight, dec_embed_bias, mask_token, dec_ln1_gain, dec_ln1_shift, dec_qkv_weight,
    dec_qv_bias, dec_out_weight, dec_out_bias, dec_ln2_gain, dec_ln2_shift, dec_up_weight,
    dec_up_bias, dec_down_weight, cotangent,
):
    pipe = lax.axis_index("z_lo")
    items, patches, half_pix = pixels.shape
    bands_here = running_mean.shape[0]
    band_pix = half_pix // bands_here
    width, dec_width = patch_weight.shape[1], dec_embed_weight.shape[1]

    vector = join((
        patch_bias, enc_ln1_gain, enc_ln1_shift, enc_out_bias, enc_ln2_gain, enc_ln2_shift, enc_down_bias,
        enc_qv_bias, enc_up_bias, dec_embed_bias, mask_token, dec_ln1_gain, dec_ln1_shift, dec_out_bias,
        dec_ln2_gain, dec_ln2_shift, dec_qv_bias, dec_up_bias))
    enc_part, vector = gather_enc(
        jnp.concatenate([enc_qkv_weight, enc_out_weight, dec_embed_weight], axis=1), enc_up_weight,
        enc_down_weight, vector)
    patch_rows, stats = gather_patch(patch_weight, after(band_sums(pixels, bands_here), vector))
    dec_part, vectors = gather_dec(
        jnp.concatenate([dec_qkv_weight, dec_out_weight], axis=1), dec_up_weight, dec_down_weight, vector,
        stats)
    enc_s, enc_qv, enc_upb, dec_s, dec_qv, dec_upb = spread(vectors)
    enc_qv, enc_upb, dec_qv, dec_upb = enc_qv[0], enc_upb[0], dec_qv[0], dec_upb[0]
    band_view = pixels.reshape(items, patches, bands_here, band_pix)
    band_total, band_square = stats
    population = 64 * items * patches * band_pix
    band_mean = band_total / population
    band_var = band_square / population - band_mean * band_mean
    band_scale = lax.rsqrt(band_var + band_epsilon)
    band_means = 0.9 * running_mean + 0.1 * band_mean
    band_variances = 0.9 * running_var + 0.1 * band_var
    normalized = ((band_view - band_mean[:, None]) * band_scale[:, None]).reshape(items, patches, half_pix)

    index = jnp.pad(visible_index, ((0, 0), (0, SLOTS - visible_index.shape[1])))
    keep = jnp.arange(SLOTS)[None, :] < visible_counts[:, None]
    onehot = (
        (index[:, :, None] == jnp.arange(GRID)[None, None, :]) & keep[:, :, None]
    ).astype(BF16)
    picked = jnp.einsum("ivp,iph->ivh", onehot[:, :, :patches], normalized.astype(BF16),
                        preferred_element_type=F32).astype(BF16)
    embedded = jnp.einsum("ivh,hd->ivd", picked, patch_rows, preferred_element_type=F32).astype(BF16)
    embedded, dec_part = together(embedded, dec_part)
    other_half = swap(take(embedded, 1 - pipe), "z_lo")
    start_rows = (
        take(embedded, pipe).astype(F32) + other_half.astype(F32) + enc_s[0] + position_rows(take(index, pipe), width)
    )
    dec_pos = position_rows(jnp.arange(GRID), dec_width)
    ring = [dec_part, shift(dec_part, "y", 1, True)]
    enc_part, start_rows, ring[1], dec_pos = together(enc_part, start_rows, ring[1], dec_pos)
    ring.append(shift(ring[1], "y", 1, True))
    enc_weights = list(unpack_enc(enc_part))
    enc_weights[0], ring[2] = together(enc_weights[0], ring[2])
    enc_qkv, enc_out, embed, enc_up, enc_down = enc_weights
    ring.append(shift(ring[2], "y", 1, True))
    dec_qkv, dec_out, dec_up, dec_down = unpack_dec(ring, [swap(block, "core") for block in ring])
    encoder = (enc_s[1], enc_s[2], enc_qkv, enc_qv, enc_out, enc_s[3], enc_s[4], enc_s[5], enc_up, enc_upb,
               enc_down, enc_s[6])
    decoder = (dec_s[2], dec_s[3], dec_qkv, dec_qv, dec_out, dec_s[4], dec_s[5], dec_s[6], dec_up, dec_upb,
               dec_down, jnp.zeros((dec_width,), F32))
    my_onehot = take(onehot, pipe)
    my_count = lax.dynamic_slice_in_dim(visible_counts, pipe, 1)
    start_rows = (
        take(embedded, pipe).astype(F32) + other_half.astype(F32) + enc_s[0] + position_rows(take(index, pipe), width)
    )
    hidden, active, enc_stored = block_forward(start_rows, encoder, HEADS, my_count)
    encoded = (hidden + (dot(active, enc_down) + encoder[11])).astype(BF16)
    latent = (dot(encoded, embed) + dec_s[0]).astype(BF16)
    covered = jnp.sum(my_onehot.astype(F32), axis=0)
    bare = jnp.where(jnp.arange(GRID) < patches, 1.0 - covered, 0.0)[:, None]
    grid = t_dot(my_onehot, latent) + bare * dec_s[1] + dec_pos
    grid_count = jnp.full((1,), patches, jnp.int32)
    _, _, dec_stored = block_forward(grid, decoder, DHEADS, grid_count)
    target = jnp.pad(take(cotangent, pipe), ((0, GRID - patches), (0, 0)))
    shape_d, shape_a, shape_b = (2, 4, 2, 2, 384, 256), (2, 4, 2, 2, 336, 256), (2, 4, 2, 2, 576, 256)
    sent = {}

    def send_dec(name, lhs, rhs):
        if name in ("gelu", "attended"):
            return rhs
        if name == "qkv":
            sent["d"] = wide_grad(lhs, rhs, sent["d"], shape_d, "xz", 32, 0, 0, 4)
            return rhs
        place = {"down": (128, 2, 0, 1), "up": (32, 4, 0, 4), "out": (32, 0, 6, 4)}[name]
        sent["d"] = wide_grad(lhs, rhs[None], sent.get("d"), shape_d, "xz", *place)
        return rhs

    grid_grad, (dg1, ds1, dob, dg2, ds2, _), dqv, dub = block_backward(
        target, dec_stored, decoder, DHEADS, grid_count, send_dec)
    mask_grad = jnp.sum(bare * grid_grad, axis=0)
    latent_grad = dot(my_onehot, grid_grad.astype(BF16)).astype(BF16)
    embed_bias_grad = jnp.sum(latent_grad.astype(F32), axis=0)
    encoded_grad = dot_t(latent_grad, embed).astype(BF16).astype(F32)
    encoded_grad = hold(encoded_grad, sent["d"])
    part_d = core_got(sent["d"])

    def send_enc(name, lhs, rhs):
        if name == "down":
            sent["feed"] = tall_grad(lhs, rhs, shape_b)
        if name == "up":
            sent["feed"] = wide_grad(lhs, rhs[None], sent["feed"], shape_b, "xz", 48, 6, 0, 6)
            rhs = hold(rhs, sent["feed"])
            sent["feed"] = core_got(sent["feed"])
        if name == "out":
            part = wide_grad(encoded, latent_grad[None], None, shape_a, "xz", 48, 0, 12, 7)
            sent["a"] = wide_grad(lhs, rhs[None], part, shape_a, "xz", 48, 0, 9, 7)
        if name == "attended":
            rest = add_cores(part_d, sent["feed"], rhs)
            rhs = hold(rhs, rest)
            sent["rest"] = lax.psum_scatter(rest.reshape(-1, 256), ("x", "z_hi", "z_lo"), tiled=True)
        if name == "qkv":
            part = wide_grad(lhs, rhs, sent["a"], shape_a, "xz", 48, 0, 0, 7)
            rhs = hold(rhs, part)
            sent["a"] = core_sum(part)
        return rhs

    start_grad, (eg1, es1, eob, eg2, es2, edb), eqv, eub = block_backward(
        encoded_grad, enc_stored, encoder, HEADS, my_count, send_enc)
    start_low = hold(start_grad.astype(BF16), sent["a"])
    start_other = swap(start_low, "z_lo")
    arrived = lax.all_to_all(sent["a"].reshape(16, 336, 256), ("x", "z_hi", "z_lo"), 0, 0)
    blocks = by_row(arrived, sent["rest"])
    patch_bias_grad = jnp.sum(start_low.astype(F32), axis=0)
    start_pair = jnp.where(pipe == 0, jnp.stack([start_low, start_other]), jnp.stack([start_other, start_low]))
    vector_grads = collect(
        patch_bias_grad, eg1, es1, eob, eg2, es2, edb, eqv, eub,
        embed_bias_grad, mask_grad, dg1, ds1, dob, dg2, ds2, dqv, dub)
    out_patch, ev, dv = sum_patch(
        t_dot(picked.reshape(-1, half_pix), start_pair.reshape(-1, width)),
        vector_grads.reshape(2, 4, 2, 4, 2, 2, 128), blocks)
    start_pair = hold(start_pair, blocks)
    picked_grad = jnp.einsum("ivd,hd->ivh", start_pair, patch_rows, preferred_element_type=F32).astype(BF16)
    pixel_grad = place_pixels(onehot, picked_grad, jnp.repeat(band_scale, band_pix)[None], patches)
    out6, out_up, out_down, out4, out_dup, out_ddown = sum_over_y(blocks)
    return (
        band_means, band_variances, pixel_grad, out_patch, ev[:6], ev[6:12], ev[12:18],
        out6[:, : 3 * width], ev[42:54], out6[:, 3 * width : 4 * width], ev[18:24], ev[24:30], ev[30:36],
        out_up, ev[54:78], out_down, ev[36:42], out6[:, 4 * width :], dv[:4], dv[4:8], dv[8:12], dv[12:16],
        out4[:, : 3 * dec_width], dv[28:36], out4[:, 3 * dec_width :], dv[16:20], dv[20:24], dv[24:28],
        out_dup, dv[36:52], out_ddown,
    )


def solution(mesh):
    whole = P(ALL)
    sizes = (2, 4, 2, 4, 2)
    cube = Mesh(mesh.devices.reshape(sizes), ALL)
    placed = (P(DP, None, "z_lo"), P(DP), P(DP, None), P("z_lo"), P("z_lo")) + (whole,) * 28 + (P(DP, None, None),)
    return jax.shard_map(
        per_device,
        mesh=cube,
        in_specs=placed,
        out_specs=(P("z_lo"), P("z_lo"), P(DP, None, "z_lo")) + (whole,) * 28,
        check_vma=False,
    )
```

```python
import functools
import math

import jax
import jax.numpy as jnp
from jax import lax
from jax.experimental import pallas as pl
from jax.experimental.pallas import tpu as pltpu
from jax.sharding import Mesh
from jax.sharding import PartitionSpec as P

HEADS = 12
DHEADS = 16
SLOTS = 256
GRID = 592

band_epsilon = 1e-05
norm_epsilon = 1e-06
masked_score = -1e30
LOG2E = 1.4426950408889634

PIPE = ("z_lo",)
DP = ("x", "z_hi", "y", "core")
ALL = PIPE + DP
RING = {"x": ("x",), "y": ("y",), "z": ("z_lo", "z_hi")}
F32 = jnp.float32
BF16 = jnp.bfloat16


def along(axis, place):
    return (place % 2) * 2 + place // 2 if axis == "z" else place


def ring_place(axis):
    if axis == "z":
        return lax.axis_index("z_hi") * 2 + lax.axis_index("z_lo")
    return lax.axis_index(axis)


def shift(value, axis, step, mirrored):
    pairs = []
    for place in range(4):
        for core in range(2):
            target = (place + (-step if mirrored and core else step)) % 4
            pairs.append((along(axis, place) * 2 + core, along(axis, target) * 2 + core))
    return lax.ppermute(value, RING[axis] + ("core",), pairs)


def swap(value, axis):
    return lax.ppermute(value, axis, [(0, 1), (1, 0)])


def put(blocks, block, index):
    return lax.dynamic_update_slice_in_dim(blocks, block[None], index, axis=0)


def take(blocks, index):
    return lax.dynamic_index_in_dim(blocks, index, axis=0, keepdims=False)


def direction():
    return jnp.where(lax.axis_index("core") == 0, 1, 3)


def by_core(mine, other):
    first = lax.axis_index("core") == 0
    return jnp.where(first, mine, other), jnp.where(first, other, mine)


def halves(array):
    rows, columns = array.shape
    return array.reshape(rows, 2, columns // 2).transpose(1, 0, 2)


def chunks(array, width):
    *lead, rows, columns = array.shape
    count = columns // width
    cut = jnp.moveaxis(array.reshape(*lead, rows, count, width), -2, -3)
    return cut.reshape(*lead, count * rows, width)


def pad_rows(array, rows):
    return jnp.pad(array, ((0, rows - array.shape[0]), (0, 0)))


def share(block, axes):
    count = lax.axis_size(axes)
    spread = jnp.broadcast_to(block[None], (count,) + block.shape)
    return lax.all_to_all(spread, axes, 0, 0)


def ring_share(block, axis):
    back = [shift(block, axis, step, False) for step in (3, 2, 1)] + [block]
    return lax.dynamic_slice_in_dim(jnp.stack(back + back[:3]), 3 - ring_place(axis), 4)


def sum_shares(blocks, axes):
    return jnp.sum(lax.all_to_all(blocks, axes, 0, 0).astype(F32), axis=0)


def after(value, *earlier):
    return lax.optimization_barrier((value,) + earlier)[0]


def join_kernel(*refs):
    ins, out = refs[:-1], refs[-1]
    for side in range(2):
        rows = [r[...].astype(F32).reshape(1, -1) for r in ins[side * 9 : side * 9 + 9]]
        rows.append(jnp.zeros((1, 128 - sum(r.shape[1] for r in rows)), F32))
        out[:, side * 128 : side * 128 + 128] = jnp.concatenate(rows, axis=1).astype(BF16)


def join(vectors):
    return pl.pallas_call(join_kernel, out_shape=jax.ShapeDtypeStruct((1, 256), BF16))(*vectors)


def in_hbm(array):
    return pltpu.with_memory_space_constraint(array, pltpu.HBM)


def made_in(shape):
    return pltpu.HBM(shape, BF16) if shape[-2] in (336, 576) else jax.ShapeDtypeStruct(shape, BF16)


def core_id():
    return lax.axis_index("core").astype(jnp.int32).reshape(1)


def direct_sum(blocks, axis):
    me = ring_place(axis)
    total = take(blocks, me).astype(F32)
    for step in (1, 2, 3):
        total = total + shift(take(blocks, (me + step) % 4), axis, step, False).astype(F32)
    return total.astype(BF16)


def together(*values):
    return lax.optimization_barrier(values)


def held_kernel(value, *rest):
    pass


def hold(value, *earlier):
    anywhere = pl.BlockSpec(memory_space=pl.ANY)
    large = pl.BlockSpec(memory_space=pltpu.HBM)
    return pl.pallas_call(
        held_kernel,
        out_shape=jax.ShapeDtypeStruct(value.shape, value.dtype),
        in_specs=[anywhere] + [large if e.shape[-2:] in ((336, 256), (576, 256), (960, 256)) else anywhere for e in earlier],
        out_specs=anywhere,
        input_output_aliases={0: 0},
    )(value, *earlier)


def on_each_core(core_ref, mine, other, work):
    @pl.when(core_ref[0] == 0)
    def _():
        work((mine, other))

    @pl.when(core_ref[0] != 0)
    def _():
        work((other, mine))


def pack_enc_kernel(raw, out):
    def rows_of(first, last, rows):
        return [raw[y, c, :, first:last].astype(F32)[:rows] for y in range(4) for c in range(2)]

    for j in range(13):
        at = j * 48
        out[at : at + 48, :] = jnp.concatenate(rows_of(j * 256, j * 256 + 256, 6), axis=0).astype(BF16)
    parts = []
    for y in range(4):
        for c in range(2):
            for g in range(3):
                parts.append(raw[y, c, :, 3328 + g * 384 : 3712 + g * 384].astype(F32))
    down = jnp.concatenate(parts, axis=0).astype(BF16)
    out[624:816, :] = down[:, :256]
    out[816:912, :128] = down[:96, 256:]
    out[816:912, 128:] = down[96:, 256:]


def pack_enc(raw):
    return pl.pallas_call(
        pack_enc_kernel,
        out_shape=jax.ShapeDtypeStruct((912, 256), BF16),
        compiler_params=pltpu.CompilerParams(vmem_limit_bytes=24 << 20),
    )(raw)


def unpack_call(kernel, part, block, index, outs):
    return pl.pallas_call(
        kernel,
        out_shape=[jax.ShapeDtypeStruct(o, BF16) for o in outs],
        grid_spec=pltpu.PrefetchScalarGridSpec(
            num_scalar_prefetch=1,
            grid=(2, 4),
            in_specs=[pl.BlockSpec(block, index)] * 2,
            out_specs=[pl.BlockSpec((o[0] // 8, o[1]), lambda zl, x, c: (zl * 4 + x, 0)) for o in outs],
        ),
        compiler_params=pltpu.CompilerParams(vmem_limit_bytes=40 << 20),
    )(core_id(), in_hbm(part), in_hbm(swap(part, "core")))


def unpack_enc_kernel(core_ref, mine, other, qkv, out, embed, up, down):
    def work(sides):
        for zh in range(2):
            rows = slice(zh * 48, zh * 48 + 48)
            for j in range(14):
                at = j % 7 * 48
                value = sides[j // 7][0, zh, 0, at : at + 48, :]
                target, k = (qkv, j) if j < 9 else (out, j - 9) if j < 12 else (embed, j - 12)
                target[rows, k * 256 : k * 256 + 256] = value
            for j in range(12):
                at = 336 + j % 6 * 48
                up[rows, j * 256 : j * 256 + 256] = sides[j // 6][0, zh, 0, at : at + 48, :]
            for side in range(2):
                ref, at, k = sides[side], side * 384, zh * 192
                down[k : k + 192, at : at + 256] = ref[0, zh, 0, 624:816, :]
                down[k : k + 96, at + 256 : at + 384] = ref[0, zh, 0, 816:912, :128]
                down[k + 96 : k + 192, at + 256 : at + 384] = ref[0, zh, 0, 816:912, 128:]

    on_each_core(core_ref, mine, other, work)


def unpack_enc(part):
    outs = [(768, 2304), (768, 768), (768, 512), (768, 3072), (3072, 768)]
    return unpack_call(
        unpack_enc_kernel, part, (1, 2, 1, 912, 256), lambda zl, x, c: (x, 0, zl, 0, 0), outs)


def unpack_dec_kernel(place_ref, *refs):
    blocks, (qkv, out, up, down, wide) = (refs[:4], refs[4:8]), refs[8:]
    for which in range(2):
        side = place_ref[0] if which == 0 else 1 - place_ref[0]
        for step in range(4):
            y = lax.rem(place_ref[1] + jnp.where(side == 0, 4 - step, step), 4)
            for zh in range(2):
                ref, k = blocks[which][step], zh * 4 + y
                values = ref[0, zh, 0, 0:64, :].astype(F32)
                for j in range(8):
                    wide[pl.ds(pl.multiple_of(k * 8, 8), 8), j * 256 : j * 256 + 256] = values[j * 8 : j * 8 + 8]
                down[
                    pl.ds(pl.multiple_of(k * 32, 32), 32), pl.ds(pl.multiple_of(side * 256, 256), 256)
                ] = ref[0, zh, 0, 64:96, :]

        def store(number):
            whole = wide[...].astype(BF16)
            if number == 0:
                qkv[:, :1024] = whole[:, :1024]
            else:
                qkv[:, 1024:] = whole[:, :512]
                out[...] = whole[:, 512:1024]
            up[:, number * 1024 : number * 1024 + 1024] = whole[:, 1024:]

        pl.when(side == 0)(functools.partial(store, 0))
        pl.when(side == 1)(functools.partial(store, 1))


def unpack_dec(mine, other):
    outs = [(512, 1536), (512, 512), (512, 2048), (2048, 512)]
    place = jnp.stack([lax.axis_index("core"), ring_place("y")]).astype(jnp.int32)
    return pl.pallas_call(
        unpack_dec_kernel,
        out_shape=[jax.ShapeDtypeStruct(o, BF16) for o in outs],
        grid_spec=pltpu.PrefetchScalarGridSpec(
            num_scalar_prefetch=1,
            grid=(2, 4),
            in_specs=[pl.BlockSpec((1, 2, 1, 96, 256), lambda zl, x, c: (x, 0, zl, 0, 0))] * 8,
            out_specs=[pl.BlockSpec((o[0] // 8, o[1]), lambda zl, x, c: (zl * 4 + x, 0)) for o in outs],
            scratch_shapes=[pltpu.VMEM((64, 2048), F32)],
        ),
        compiler_params=pltpu.CompilerParams(vmem_limit_bytes=40 << 20),
    )(place, *mine, *other)


def cut(array):
    both = halves(array)
    core = lax.axis_index("core")
    return take(both, core), take(both, 1 - core)


def gather_enc(enc6, enc_up, enc_down, vector):
    def enc(which):
        rows = [pad_rows(p, 8) for p in (cut(enc6)[which], cut(enc_up)[which])]
        tall = cut(enc_down)[which].reshape(3, 8, -1).transpose(1, 0, 2).reshape(8, -1)
        return jnp.concatenate(rows + [tall, pad_rows(cut(vector)[which], 8)], axis=1)

    raw = jnp.stack(by_core(enc(0), swap(enc(1), "core")))
    raw = ring_share(raw, "y")
    part = lax.all_gather(pack_enc(raw), ("x", "z_hi", "z_lo"), tiled=False).reshape(4, 2, 2, 912, 256)
    return part, raw[:, :, 0, 4480:].reshape(8, 128)


def gather_patch(patch, stats):
    mine, other = cut(patch)
    rows = jnp.concatenate(by_core(mine, swap(other, "core")), axis=0)
    flat = stats.reshape(1, -1)
    high = lax.reduce_precision(flat, 8, 7)
    mid = lax.reduce_precision(flat - high, 8, 7)
    three = jnp.concatenate([high, mid, flat - high - mid], axis=0)
    three = jnp.pad(three, ((0, 5), (0, rows.shape[1] - three.shape[1]))).astype(BF16)
    blocks = share(jnp.concatenate([rows, three], axis=0), ("x", "z_hi", "y"))
    stats = jnp.sum(blocks[:, 24:27, : flat.shape[1]].astype(F32), axis=(0, 1)).reshape(stats.shape)
    rows = blocks[:, :24].reshape(-1, rows.shape[1])
    return jnp.concatenate(by_core(rows, swap(rows, "core")), axis=1), stats


def gather_dec(dec4, dec_up, dec_down, vectors, started):
    def dec(which):
        wide = jnp.concatenate([cut(dec4)[which], cut(dec_up)[which]], axis=1)
        return wide, cut(dec_down)[which]

    mine, other = dec(0), dec(1)
    wide = jnp.concatenate(by_core(mine[0], swap(other[0], "core")), axis=0)
    tall = jnp.concatenate(by_core(mine[1], swap(other[1], "core")), axis=0)
    vectors = jnp.pad(vectors, ((0, 0), (0, 128)))
    part = after(jnp.concatenate([chunks(wide, 256), tall, vectors], axis=0), started)
    part = share(part, ("x", "z_hi", "z_lo"))
    vectors = part[:, 96:, :128].reshape(128, 128)
    low, high = by_core(vectors, swap(vectors, "core"))
    return part[:, :96].reshape(4, 2, 2, 96, 256), jnp.concatenate([low, high], axis=1)


def spread_kernel(vectors, *outs):
    values = vectors[...]
    for side, unit in ((0, 6), (1, 4)):
        for k, (times, first, count) in enumerate(((1, 0, 7), (2, 7, 1), (4, 9, 1))):
            size = unit * times
            length = size * 128
            place = lax.broadcasted_iota(jnp.int32, (128, length), 1)
            row = lax.broadcasted_iota(jnp.int32, (128, length), 0)
            device = (row & 8) * 8 + (row >> 5) * 16 + (row & 16) // 2 + (row & 7)
            lifted = (place >= device * size) & (place < device * size + size)
            table = lax.dot_general(
                values[:, side * 128 : side * 128 + 128], lifted.astype(BF16),
                (((0,), (0,)), ((), ())), preferred_element_type=F32)
            inside = place[:1] - lax.div(place[:1], size) * size
            for n in range(count):
                wanted = row == inside + (first + n) * unit
                outs[side * 3 + k][n : n + 1, :] = jnp.sum(jnp.where(wanted, table, 0.0), axis=0, keepdims=True)


def spread(vectors):
    shapes = [(8, 768), (1, 1536), (1, 3072), (8, 512), (1, 1024), (1, 2048)]
    return pl.pallas_call(
        spread_kernel,
        out_shape=[jax.ShapeDtypeStruct(s, F32) for s in shapes],
        compiler_params=pltpu.CompilerParams(vmem_limit_bytes=24 << 20),
    )(vectors)


def collect_kernel(*refs):
    ins, out = refs[:-1], refs[-1]
    for side, unit in ((0, 6), (1, 4)):
        total = jnp.zeros((128, 128), F32)
        for k, (times, first, count) in enumerate(((1, 0, 7), (2, 7, 1), (4, 9, 1))):
            size = unit * times
            length = size * 128
            place = lax.broadcasted_iota(jnp.int32, (128, length), 1)
            row = lax.broadcasted_iota(jnp.int32, (128, length), 0)
            lifted = (place >= row * size) & (place < row * size + size)
            inside = place[:1] - lax.div(place[:1], size) * size
            table = jnp.zeros((128, length), F32)
            for n in range(count):
                given = ins[side * 9 + n + (0, 7, 8)[k]][...].reshape(1, -1)
                table = jnp.where(row == inside + (first + n) * unit, given, table)
            total = total + lax.dot_general(
                lifted.astype(BF16), table.astype(BF16), (((1,), (1,)), ((), ())), preferred_element_type=F32)
        out[:, side * 128 : side * 128 + 128] = total.astype(BF16)


def collect(*vectors):
    return pl.pallas_call(
        collect_kernel,
        out_shape=jax.ShapeDtypeStruct((128, 256), BF16),
        compiler_params=pltpu.CompilerParams(vmem_limit_bytes=24 << 20),
    )(*vectors)


def wide_grad_kernel(order, rows, lhs, rhs, *rest):
    out, turned = rest[-2:]

    @pl.when(pl.program_id(0) == 0)
    def _():
        turned[...] = lhs[...].T

    result = jnp.dot(turned[...], rhs[0], preferred_element_type=F32).astype(BF16)
    for block in range(16):
        zl, x, zh = block // 8, block // 2 % 4, block % 2
        spot = (0, x, zh, zl) if order == "xz" else (0, zh, zl, x)
        out[spot] = result[block * rows : block * rows + rows]


def wide_grad(lhs, rhs, buffer, shape, order, rows, row_block, first, per_side):
    length, height = lhs.shape
    parts, _, width = rhs.shape
    per_part = width // 256
    block = (1, 4, 2, 2, rows, 256) if order == "xz" else (1, 2, 2, 4, rows, 256)

    def place(j):
        chunk = j + first
        return (chunk // per_side, 0, 0, 0, row_block + chunk % per_side, 0)

    given = () if buffer is None else (buffer,)
    return pl.pallas_call(
        functools.partial(wide_grad_kernel, order, rows),
        out_shape=made_in(shape),
        grid=(parts * per_part,),
        in_specs=[
            pl.BlockSpec((length, height), lambda j: (0, 0)),
            pl.BlockSpec((1, length, 256), lambda j: (j // per_part, 0, j % per_part)),
        ] + [pl.BlockSpec(memory_space=pltpu.HBM if shape[-2] in (336, 576) else pl.ANY)] * len(given),
        out_specs=pl.BlockSpec(block, place),
        scratch_shapes=[pltpu.VMEM((height, length), BF16)],
        input_output_aliases={2: 0} if given else {},
        compiler_params=pltpu.CompilerParams(vmem_limit_bytes=40 << 20),
        cost_estimate=pl.CostEstimate(
            flops=2 * length * height * width * parts, transcendentals=0,
            bytes_accessed=2 * (length * height + parts * length * width + parts * height * width)),
    )(lhs, rhs, *given)


def tall_grad_kernel(lhs, rhs, out, turned):
    @pl.when(pl.program_id(0) == 0)
    def _():
        turned[...] = lhs[...].T

    result = jnp.dot(turned[...], rhs[...], preferred_element_type=F32).astype(BF16)
    for block in range(16):
        zl, x, zh = block // 8, block // 2 % 4, block % 2
        out[0, x, zh, zl, :, :128] = result[block * 192 : block * 192 + 96]
        out[0, x, zh, zl, :, 128:] = result[block * 192 + 96 : block * 192 + 192]


def tall_grad(lhs, rhs, shape):
    length, height = lhs.shape
    return pl.pallas_call(
        tall_grad_kernel,
        out_shape=made_in(shape),
        grid=(6,),
        in_specs=[pl.BlockSpec((length, height), lambda j: (0, 0)), pl.BlockSpec((length, 128), lambda j: (0, j))],
        out_specs=pl.BlockSpec((1, 4, 2, 2, 96, 256), lambda j: (j // 3, 0, 0, 0, j % 3, 0)),
        scratch_shapes=[pltpu.VMEM((height, length), BF16)],
        compiler_params=pltpu.CompilerParams(vmem_limit_bytes=40 << 20),
        cost_estimate=pl.CostEstimate(
            flops=2 * length * height * rhs.shape[1], transcendentals=0, bytes_accessed=4 * height * rhs.shape[1]),
    )(lhs, rhs)


def add_cores_kernel(info, *refs):
    out = refs[-1]
    at = 0
    for mine, got in zip(refs[0:4:2], refs[1:4:2], strict=True):
        rows = got.shape[1]
        out[0, at : at + rows, :] = (mine[0, 0].astype(F32) + got[0].astype(F32)).astype(BF16)
        at += rows


def add_cores(first, second, *earlier):
    core = lax.axis_index("core")
    operands, specs, rows = [], [], 0
    for part, got in (first, second):
        count = part.shape[-2]
        operands += [in_hbm(part.reshape(2, 16, count, 256)), in_hbm(got.reshape(16, count, 256))]
        specs += [
            pl.BlockSpec((1, 1, count, 256), lambda i, info: (info[0], i, 0, 0)),
            pl.BlockSpec((1, count, 256), lambda i, info: (i, 0, 0))]
        rows += count
    return pl.pallas_call(
        add_cores_kernel,
        out_shape=pltpu.HBM((16, rows, 256), BF16),
        grid_spec=pltpu.PrefetchScalarGridSpec(
            num_scalar_prefetch=1,
            grid=(16,),
            in_specs=specs + [pl.BlockSpec(memory_space=pl.ANY)] * len(earlier),
            out_specs=pl.BlockSpec((1, rows, 256), lambda i, info: (i, 0, 0)),
        ),
        compiler_params=pltpu.CompilerParams(vmem_limit_bytes=24 << 20),
    )(core.astype(jnp.int32).reshape(1), *operands, *earlier)


def core_got(part):
    return part, swap(take(part, 1 - lax.axis_index("core")), "core")


def core_sum(part):
    core = lax.axis_index("core")
    got = swap(take(part, 1 - core), "core")
    return (take(part, core).astype(F32) + got.astype(F32)).astype(BF16)


def finish(mine, other):
    return by_core(mine, swap(other, "core"))


def finish_pair(pair):
    core = lax.axis_index("core")
    return finish(take(pair, core), take(pair, 1 - core))


def join_columns(sides, first, last, rows):
    return jnp.concatenate([side[:rows, first:last] for side in sides], axis=1).astype(F32)


def by_row_kernel(arrived, rest, out):
    last = jnp.zeros((336, 256), F32)
    for block in range(16):
        last = last + arrived[block].astype(F32)
    rest = rest[...].astype(F32)
    out[...] = jnp.zeros_like(out)

    def chunk(value, at, rows):
        for k in range(8):
            out[k // 2, k % 2, 0:rows, at : at + 256] = value[k * rows : (k + 1) * rows].astype(BF16)

    for j in range(7):
        chunk(last[j * 48 : j * 48 + 48], j * 256, 6)
    for j in range(6):
        chunk(rest[672 + j * 48 : 720 + j * 48], 1792 + j * 256, 6)
    for k in range(8):
        y, c = k // 2, k % 2
        for g in range(3):
            for j in range(3):
                n = k % 4 * 24 + g * 8
                value = rest[384 + j * 96 + n : 392 + j * 96 + n, k // 4 * 128 : k // 4 * 128 + 128]
                at = 3328 + g * 384 + j * 128
                out[y, c, :, at : at + 128] = value.astype(BF16)
        for j in range(4):
            n = j * 32 + k * 4
            value = jnp.concatenate([rest[n : n + 4], rest[n + 128 : n + 132]], axis=0)
            out[y, c, :, 4480 + j * 256 : 4736 + j * 256] = value.astype(BF16)
        for g in range(2):
            n = 256 + k * 16 + g * 8
            out[y, c, :, 5504 + g * 256 : 5760 + g * 256] = rest[n : n + 8].astype(BF16)


def by_row(arrived, rest):
    return pl.pallas_call(
        by_row_kernel,
        out_shape=jax.ShapeDtypeStruct((4, 2, 8, 6016), BF16),
        compiler_params=pltpu.CompilerParams(vmem_limit_bytes=40 << 20),
    )(arrived, rest)


def outputs_kernel(low, high, qkv, out, embed, up, down, dqkv, dout, dup, ddown):
    for side, ref in ((0, low), (1, high)):
        value = ref[...].astype(F32)
        if side == 0:
            qkv[:, :1792] = value[:6, :1792]
            dqkv[:, :1024] = value[:4, 4480:5504]
        else:
            qkv[:, 1792:] = value[:6, :512]
            out[...] = value[:6, 512:1280]
            embed[...] = value[:6, 1280:1792]
            dqkv[:, 1024:] = value[:4, 4480:4992]
            dout[...] = value[:4, 4992:5504]
        up[:, side * 1536 : side * 1536 + 1536] = value[:6, 1792:3328]
        for g in range(3):
            down[g * 8 : g * 8 + 8, side * 384 : side * 384 + 384] = value[:, 3328 + g * 384 : 3712 + g * 384]
        dup[:, side * 1024 : side * 1024 + 1024] = value[4:, 4480:5504]
        for g in range(2):
            ddown[g * 8 : g * 8 + 8, side * 256 : side * 256 + 256] = value[:, 5504 + g * 256 : 5760 + g * 256]


def outputs(low, high):
    shapes = [(6, 2304), (6, 768), (6, 512), (6, 3072), (24, 768), (4, 1536), (4, 512), (4, 2048), (16, 512)]
    return pl.pallas_call(
        outputs_kernel,
        out_shape=[jax.ShapeDtypeStruct(s, F32) for s in shapes],
        compiler_params=pltpu.CompilerParams(vmem_limit_bytes=24 << 20),
    )(low, high)


def sum_over_y(blocks):
    core = lax.axis_index("core")
    pair = sum_shares(blocks, "y").astype(BF16)
    return outputs(*finish(take(pair, core), take(pair, 1 - core)))


def sum_patch(rows, vectors, earlier):
    pipe = lax.axis_index("z_lo")
    got = swap(take(vectors, 1 - pipe), "z_lo")
    vectors = (take(vectors, pipe).astype(F32) + got.astype(F32)).astype(BF16)
    vectors = vectors.transpose(4, 2, 1, 0, 3, 5)[..., None, :]
    vectors = jnp.pad(vectors, ((0, 0),) * 5 + ((0, 3), (0, 256)))
    rows = rows.astype(BF16).reshape(4, 2, 4, 2, 12, 2, 384).transpose(5, 2, 1, 0, 3, 4, 6)
    part = core_sum(jnp.concatenate([rows, vectors], axis=5))
    part = direct_sum(part, "y")
    zh = lax.axis_index("z_hi")
    got = swap(take(part, 1 - zh), "z_hi")
    part = (take(part, zh).astype(F32) + got.astype(F32)).astype(BF16)
    low, high = finish_pair(direct_sum(hold(part, earlier), "x"))
    return join_columns((low, high), 0, 384, 12), low[12, :128].astype(F32), high[12, :128].astype(F32)


def layer_norm(residual, gain, shift_row):
    center = residual - jnp.mean(residual, axis=-1, keepdims=True)
    spread = jnp.mean(center * center, axis=-1, keepdims=True)
    return center * lax.rsqrt(spread + norm_epsilon) * gain + shift_row


def frequencies(model_width):
    half_width = model_width // 2
    return jnp.exp(jnp.arange(half_width).astype(F32) * (-math.log(10000.0) / half_width))


def position_rows(places, model_width):
    phase_angle = places.astype(F32)[:, None] * frequencies(model_width)[None, :]
    return jnp.concatenate([jnp.sin(phase_angle), jnp.cos(phase_angle)], axis=1)


def dot(left, right):
    return jnp.dot(left, right, preferred_element_type=F32)


def dot_t(left, right):
    return lax.dot_general(left, right, (((1,), (1,)), ((), ())), preferred_element_type=F32)


def t_dot(left, right):
    return lax.dot_general(left, right, (((0,), (0,)), ((), ())), preferred_element_type=F32)


def attend_kernel(size, count_ref, q_ref, k_ref, v_ref, o_ref):
    length = q_ref.shape[0]
    q, k, v = q_ref[...], k_ref[...], v_ref[...]
    kept = lax.broadcasted_iota(jnp.int32, (1, length), 1) < count_ref[0]
    lane = lax.broadcasted_iota(jnp.int32, (1, 128), 1)
    total = jnp.zeros((length, 128), F32)
    for head in range(128 // size):
        mine = (lane >= head * size) & (lane < (head + 1) * size)
        scores = jnp.where(kept, dot_t(jnp.where(mine, q, jnp.zeros_like(q)), k), masked_score)
        weight = jnp.exp2((scores - jnp.max(scores, axis=1, keepdims=True)) * (size ** (-0.5) * LOG2E))
        prob = (weight * (1.0 / jnp.sum(weight, axis=1, keepdims=True))).astype(BF16)
        total = total + dot(prob, jnp.where(mine, v, jnp.zeros_like(v)))
    o_ref[...] = total.astype(BF16)

def attend(qkv, heads, count):
    length, width = qkv.shape[0], qkv.shape[1] // 3
    groups = width // 128
    spec = lambda part: pl.BlockSpec((length, 128), lambda g, c, part=part: (0, part * groups + g))
    return pl.pallas_call(
        functools.partial(attend_kernel, width // heads),
        out_shape=jax.ShapeDtypeStruct((length, width), BF16),
        grid_spec=pltpu.PrefetchScalarGridSpec(
            num_scalar_prefetch=1, grid=(groups,),
            in_specs=[spec(0), spec(1), spec(2)],
            out_specs=pl.BlockSpec((length, 128), lambda g, c: (0, g))),
        compiler_params=pltpu.CompilerParams(vmem_limit_bytes=48 << 20),
    )(count, qkv, qkv, qkv)

def attend_back_kernel(size, count_ref, q_ref, k_ref, v_ref, g_ref, o_ref, turned):
    length = q_ref.shape[0]
    q, k, v, g = q_ref[...], k_ref[...], v_ref[...], g_ref[...]
    k_turned = k.T
    kept = lax.broadcasted_iota(jnp.int32, (length, 1), 0) < count_ref[0]
    lane = lax.broadcasted_iota(jnp.int32, (1, 128), 1)
    dk = jnp.zeros((length, 128), F32)
    dv = jnp.zeros((length, 128), F32)
    zero = jnp.zeros_like(q)
    for head in range(128 // size):
        mine = (lane >= head * size) & (lane < (head + 1) * size)
        q_h, g_h = jnp.where(mine, q, zero), jnp.where(mine, g, zero)
        scores = jnp.where(kept, dot_t(k, q_h), masked_score)
        weight = jnp.exp2((scores - jnp.max(scores, axis=0, keepdims=True)) * (size ** (-0.5) * LOG2E))
        prob = weight * (1.0 / jnp.sum(weight, axis=0, keepdims=True))
        dv = dv + dot(prob.astype(BF16), g_h)
        prob_grad = dot_t(v, g_h)
        inner = jnp.sum(prob * prob_grad, axis=0, keepdims=True)
        score_grad = (prob * (prob_grad - inner)).astype(BF16)
        dk = dk + dot(score_grad, q_h)
        turned[head * size : (head + 1) * size, :] = dot(k_turned[head * size : (head + 1) * size], score_grad)
    o_ref[0] = (turned[...] * size ** (-0.5)).T.astype(BF16)
    o_ref[1] = (dk * size ** (-0.5)).astype(BF16)
    o_ref[2] = dv.astype(BF16)

def attend_back(qkv, grad, heads, count):
    length, width = qkv.shape[0], qkv.shape[1] // 3
    groups = width // 128
    spec = lambda part: pl.BlockSpec((length, 128), lambda g, c, part=part: (0, part * groups + g))
    return pl.pallas_call(
        functools.partial(attend_back_kernel, width // heads),
        out_shape=jax.ShapeDtypeStruct((3, length, width), BF16),
        grid_spec=pltpu.PrefetchScalarGridSpec(
            num_scalar_prefetch=1, grid=(groups,),
            in_specs=[spec(0), spec(1), spec(2), spec(0)],
            out_specs=pl.BlockSpec((3, length, 128), lambda g, c: (0, 0, g)),
            scratch_shapes=[pltpu.VMEM((128, length), F32)]),
        compiler_params=pltpu.CompilerParams(vmem_limit_bytes=56 << 20),
    )(count, qkv, qkv, qkv, grad)


def block_forward(residual, weights, head_count, key_keep):
    (gain1, shift1, qkv_weight, qv_bias, out_weight, out_bias, gain2, shift2, up_weight, up_bias,
     down_weight, down_bias) = weights
    width = residual.shape[1]
    normed = layer_norm(residual, gain1, shift1).astype(BF16)
    qkv_bias = jnp.concatenate([qv_bias[:width], jnp.zeros((width,), F32), qv_bias[width:]])
    qkv_rows = (dot(normed, qkv_weight) + qkv_bias).astype(BF16)
    attended = attend(qkv_rows, head_count, key_keep)
    hidden = residual + (dot(attended, out_weight) + out_bias)
    second = layer_norm(hidden, gain2, shift2).astype(BF16)
    up_proj = dot(second, up_weight) + up_bias
    active = jax.nn.gelu(up_proj).astype(BF16)
    stored = (residual, normed, qkv_rows, attended, hidden, second, up_proj, active)
    return hidden, active, stored


def block_backward(grad_out, stored, weights, head_count, key_keep, send):
    (gain1, shift1, qkv_weight, qv_bias, out_weight, out_bias, gain2, shift2, up_weight, up_bias,
     down_weight, down_bias) = weights
    (residual, normed, qkv_rows, attended, hidden, second, up_proj, active) = stored
    width = residual.shape[1]
    down_branch = grad_out.astype(BF16)
    down_bias_grad = jnp.sum(down_branch.astype(F32), axis=0)
    down_branch = send("down", active, down_branch)
    active_grad = dot_t(down_branch, down_weight)
    up_grad = send("gelu", None, jax.vjp(jax.nn.gelu, up_proj)[1](active_grad)[0].astype(BF16))
    up_bias_grad = jnp.sum(up_grad.astype(F32), axis=0)
    up_grad = send("up", second, up_grad)
    second_grad = dot_t(up_grad, up_weight)
    hidden_grad, gain2_grad, shift2_grad = jax.vjp(layer_norm, hidden, gain2, shift2)[1](second_grad)
    hidden_grad = hidden_grad + grad_out
    attn_branch = hidden_grad.astype(BF16)
    out_bias_grad = jnp.sum(attn_branch.astype(F32), axis=0)
    attn_branch = send("out", attended, attn_branch)
    attended_grad = send("attended", None, dot_t(attn_branch, out_weight).astype(BF16))
    qkv_parts = attend_back(qkv_rows, attended_grad, head_count, key_keep)
    qkv_parts = send("qkv", normed, qkv_parts)
    qkv_grad = jnp.concatenate([qkv_parts[0], qkv_parts[1], qkv_parts[2]], axis=1)
    qkv_sums = jnp.sum(qkv_grad.astype(F32), axis=0)
    qv_bias_grad = jnp.concatenate([qkv_sums[:width], qkv_sums[2 * width :]])
    normed_grad = dot_t(qkv_grad, qkv_weight)
    residual_grad, gain1_grad, shift1_grad = jax.vjp(layer_norm, residual, gain1, shift1)[1](normed_grad)
    residual_grad = residual_grad + hidden_grad
    vectors = (gain1_grad, shift1_grad, out_bias_grad, gain2_grad, shift2_grad, down_bias_grad)
    return residual_grad, vectors, qv_bias_grad, up_bias_grad


def band_sums(pixels, bands):
    items, patches, width = pixels.shape
    view = pixels.reshape(items, patches, bands, width // bands)
    sums = jnp.stack([jnp.sum(view, axis=(0, 1, 3)), jnp.sum(view * view, axis=(0, 1, 3))])
    return sums + swap(sums, "core")


def pixel_kernel(onehot, grad, scale, out):
    placed = lax.dot_general(
        onehot[0], grad[0], (((0,), (0,)), ((), ())), preferred_element_type=F32)
    out[0] = placed[: out.shape[1]] * scale[...]


def place_pixels(onehot, grad, scale, patches):
    items, slots, grid = onehot.shape
    width = grad.shape[2]
    return pl.pallas_call(
        pixel_kernel,
        out_shape=jax.ShapeDtypeStruct((items, patches, width), F32),
        grid=(items,),
        in_specs=[
            pl.BlockSpec((1, slots, grid), lambda i: (i, 0, 0)),
            pl.BlockSpec((1, slots, width), lambda i: (i, 0, 0)),
            pl.BlockSpec((1, width), lambda i: (0, 0)),
        ],
        out_specs=pl.BlockSpec((1, patches, width), lambda i: (i, 0, 0)),
        compiler_params=pltpu.CompilerParams(vmem_limit_bytes=24 << 20),
    )(onehot, grad, scale)


def per_device(
    pixels, visible_counts, visible_index, running_mean, running_var, patch_weight, patch_bias,
    enc_ln1_gain, enc_ln1_shift, enc_qkv_weight, enc_qv_bias, enc_out_weight, enc_out_bias,
    enc_ln2_gain, enc_ln2_shift, enc_up_weight, enc_up_bias, enc_down_weight, enc_down_bias,
    dec_embed_weight, dec_embed_bias, mask_token, dec_ln1_gain, dec_ln1_shift, dec_qkv_weight,
    dec_qv_bias, dec_out_weight, dec_out_bias, dec_ln2_gain, dec_ln2_shift, dec_up_weight,
    dec_up_bias, dec_down_weight, cotangent,
):
    pipe = lax.axis_index("z_lo")
    items, patches, half_pix = pixels.shape
    bands_here = running_mean.shape[0]
    band_pix = half_pix // bands_here
    width, dec_width = patch_weight.shape[1], dec_embed_weight.shape[1]

    vector = join((
        patch_bias, enc_ln1_gain, enc_ln1_shift, enc_out_bias, enc_ln2_gain, enc_ln2_shift, enc_down_bias,
        enc_qv_bias, enc_up_bias, dec_embed_bias, mask_token, dec_ln1_gain, dec_ln1_shift, dec_out_bias,
        dec_ln2_gain, dec_ln2_shift, dec_qv_bias, dec_up_bias))
    enc_part, vector = gather_enc(
        jnp.concatenate([enc_qkv_weight, enc_out_weight, dec_embed_weight], axis=1), enc_up_weight,
        enc_down_weight, vector)
    patch_rows, stats = gather_patch(patch_weight, after(band_sums(pixels, bands_here), vector))
    dec_part, vectors = gather_dec(
        jnp.concatenate([dec_qkv_weight, dec_out_weight], axis=1), dec_up_weight, dec_down_weight, vector,
        stats)
    enc_s, enc_qv, enc_upb, dec_s, dec_qv, dec_upb = spread(vectors)
    enc_qv, enc_upb, dec_qv, dec_upb = enc_qv[0], enc_upb[0], dec_qv[0], dec_upb[0]
    band_view = pixels.reshape(items, patches, bands_here, band_pix)
    band_total, band_square = stats
    population = 64 * items * patches * band_pix
    band_mean = band_total / population
    band_var = band_square / population - band_mean * band_mean
    band_scale = lax.rsqrt(band_var + band_epsilon)
    band_means = 0.9 * running_mean + 0.1 * band_mean
    band_variances = 0.9 * running_var + 0.1 * band_var
    normalized = ((band_view - band_mean[:, None]) * band_scale[:, None]).reshape(items, patches, half_pix)

    index = jnp.pad(visible_index, ((0, 0), (0, SLOTS - visible_index.shape[1])))
    keep = jnp.arange(SLOTS)[None, :] < visible_counts[:, None]
    onehot = (
        (index[:, :, None] == jnp.arange(GRID)[None, None, :]) & keep[:, :, None]
    ).astype(BF16)
    picked = jnp.einsum("ivp,iph->ivh", onehot[:, :, :patches], normalized.astype(BF16),
                        preferred_element_type=F32).astype(BF16)
    embedded = jnp.einsum("ivh,hd->ivd", picked, patch_rows, preferred_element_type=F32).astype(BF16)
    embedded, dec_part = together(embedded, dec_part)
    other_half = swap(take(embedded, 1 - pipe), "z_lo")
    start_rows = (
        take(embedded, pipe).astype(F32) + other_half.astype(F32) + enc_s[0] + position_rows(take(index, pipe), width)
    )
    dec_pos = position_rows(jnp.arange(GRID), dec_width)
    ring = [dec_part, shift(dec_part, "y", 1, True)]
    enc_part, start_rows, ring[1], dec_pos = together(enc_part, start_rows, ring[1], dec_pos)
    ring.append(shift(ring[1], "y", 1, True))
    enc_weights = list(unpack_enc(enc_part))
    enc_weights[0], ring[2] = together(enc_weights[0], ring[2])
    enc_qkv, enc_out, embed, enc_up, enc_down = enc_weights
    ring.append(shift(ring[2], "y", 1, True))
    other = [swap(block, "core") for block in ring[:2]]
    encoder = (enc_s[1], enc_s[2], enc_qkv, enc_qv, enc_out, enc_s[3], enc_s[4], enc_s[5], enc_up, enc_upb,
               enc_down, enc_s[6])
    my_onehot = take(onehot, pipe)
    my_count = lax.dynamic_slice_in_dim(visible_counts, pipe, 1)
    start_rows = (
        take(embedded, pipe).astype(F32) + other_half.astype(F32) + enc_s[0] + position_rows(take(index, pipe), width)
    )
    hidden, active, enc_stored = block_forward(start_rows, encoder, HEADS, my_count)
    ring[2:] = [hold(block, hidden) for block in ring[2:]]
    other += [swap(block, "core") for block in ring[2:]]
    dec_qkv, dec_out, dec_up, dec_down = unpack_dec(ring, other)
    decoder = (dec_s[2], dec_s[3], dec_qkv, dec_qv, dec_out, dec_s[4], dec_s[5], dec_s[6], dec_up, dec_upb,
               dec_down, jnp.zeros((dec_width,), F32))
    encoded = (hidden + (dot(active, enc_down) + encoder[11])).astype(BF16)
    latent = (dot(encoded, embed) + dec_s[0]).astype(BF16)
    covered = jnp.sum(my_onehot.astype(F32), axis=0)
    bare = jnp.where(jnp.arange(GRID) < patches, 1.0 - covered, 0.0)[:, None]
    grid = t_dot(my_onehot, latent) + bare * dec_s[1] + dec_pos
    grid_count = jnp.full((1,), patches, jnp.int32)
    _, _, dec_stored = block_forward(grid, decoder, DHEADS, grid_count)
    target = jnp.pad(take(cotangent, pipe), ((0, GRID - patches), (0, 0)))
    shape_d, shape_a, shape_b = (2, 4, 2, 2, 384, 256), (2, 4, 2, 2, 336, 256), (2, 4, 2, 2, 576, 256)
    sent = {}

    def send_dec(name, lhs, rhs):
        if name in ("gelu", "attended"):
            return rhs
        if name == "qkv":
            sent["d"] = wide_grad(lhs, rhs, sent["d"], shape_d, "xz", 32, 0, 0, 4)
            return rhs
        place = {"down": (128, 2, 0, 1), "up": (32, 4, 0, 4), "out": (32, 0, 6, 4)}[name]
        sent["d"] = wide_grad(lhs, rhs[None], sent.get("d"), shape_d, "xz", *place)
        return rhs

    grid_grad, (dg1, ds1, dob, dg2, ds2, _), dqv, dub = block_backward(
        target, dec_stored, decoder, DHEADS, grid_count, send_dec)
    mask_grad = jnp.sum(bare * grid_grad, axis=0)
    latent_grad = dot(my_onehot, grid_grad.astype(BF16)).astype(BF16)
    embed_bias_grad = jnp.sum(latent_grad.astype(F32), axis=0)
    encoded_grad = dot_t(latent_grad, embed).astype(BF16).astype(F32)
    encoded_grad = hold(encoded_grad, sent["d"])
    part_d = core_got(sent["d"])

    def send_enc(name, lhs, rhs):
        if name == "down":
            sent["feed"] = tall_grad(lhs, rhs, shape_b)
        if name == "up":
            sent["feed"] = wide_grad(lhs, rhs[None], sent["feed"], shape_b, "xz", 48, 6, 0, 6)
            rhs = hold(rhs, sent["feed"])
            sent["feed"] = core_got(sent["feed"])
        if name == "out":
            part = wide_grad(encoded, latent_grad[None], None, shape_a, "xz", 48, 0, 12, 7)
            sent["a"] = wide_grad(lhs, rhs[None], part, shape_a, "xz", 48, 0, 9, 7)
        if name == "attended":
            rest = add_cores(part_d, sent["feed"], rhs)
            rhs = hold(rhs, rest)
            sent["rest"] = lax.psum_scatter(rest.reshape(-1, 256), ("x", "z_hi", "z_lo"), tiled=True)
        if name == "qkv":
            part = wide_grad(lhs, rhs, sent["a"], shape_a, "xz", 48, 0, 0, 7)
            rhs = hold(rhs, part)
            sent["a"] = core_sum(part)
        return rhs

    start_grad, (eg1, es1, eob, eg2, es2, edb), eqv, eub = block_backward(
        encoded_grad, enc_stored, encoder, HEADS, my_count, send_enc)
    start_low = hold(start_grad.astype(BF16), sent["a"])
    start_other = swap(start_low, "z_lo")
    arrived = lax.all_to_all(sent["a"].reshape(16, 336, 256), ("x", "z_hi", "z_lo"), 0, 0)
    blocks = by_row(arrived, sent["rest"])
    patch_bias_grad = jnp.sum(start_low.astype(F32), axis=0)
    start_pair = jnp.where(pipe == 0, jnp.stack([start_low, start_other]), jnp.stack([start_other, start_low]))
    vector_grads = collect(
        patch_bias_grad, eg1, es1, eob, eg2, es2, edb, eqv, eub,
        embed_bias_grad, mask_grad, dg1, ds1, dob, dg2, ds2, dqv, dub)
    out_patch, ev, dv = sum_patch(
        t_dot(picked.reshape(-1, half_pix), start_pair.reshape(-1, width)),
        vector_grads.reshape(2, 4, 2, 4, 2, 2, 128), blocks)
    start_pair = hold(start_pair, blocks)
    picked_grad = jnp.einsum("ivd,hd->ivh", start_pair, patch_rows, preferred_element_type=F32).astype(BF16)
    pixel_grad = place_pixels(onehot, picked_grad, jnp.repeat(band_scale, band_pix)[None], patches)
    (out_qkv, out_out, out_embed, out_up, out_down, out_dqkv, out_dout, out_dup, out_ddown) = sum_over_y(blocks)
    return (
        band_means, band_variances, pixel_grad, out_patch, ev[:6], ev[6:12], ev[12:18],
        out_qkv, ev[42:54], out_out, ev[18:24], ev[24:30], ev[30:36],
        out_up, ev[54:78], out_down, ev[36:42], out_embed, dv[:4], dv[4:8], dv[8:12], dv[12:16],
        out_dqkv, dv[28:36], out_dout, dv[16:20], dv[20:24], dv[24:28],
        out_dup, dv[36:52], out_ddown,
    )


def solution(mesh):
    whole = P(ALL)
    sizes = (2, 4, 2, 4, 2)
    cube = Mesh(mesh.devices.reshape(sizes), ALL)
    placed = (P(DP, None, "z_lo"), P(DP), P(DP, None), P("z_lo"), P("z_lo")) + (whole,) * 28 + (P(DP, None, None),)
    return jax.shard_map(
        per_device,
        mesh=cube,
        in_specs=placed,
        out_specs=(P("z_lo"), P("z_lo"), P(DP, None, "z_lo")) + (whole,) * 28,
        check_vma=False,
    )
```

```python
import functools
import math

import jax
import jax.numpy as jnp
from jax import lax
from jax.experimental import pallas as pl
from jax.experimental.pallas import tpu as pltpu
from jax.sharding import Mesh
from jax.sharding import PartitionSpec as P

HEADS = 12
DHEADS = 16
SLOTS = 256
GRID = 592

band_epsilon = 1e-05
norm_epsilon = 1e-06
masked_score = -1e30
LOG2E = 1.4426950408889634

PIPE = ("z_lo",)
DP = ("x", "z_hi", "y", "core")
ALL = PIPE + DP
RING = {"x": ("x",), "y": ("y",), "z": ("z_lo", "z_hi")}
F32 = jnp.float32
BF16 = jnp.bfloat16


def along(axis, place):
    return (place % 2) * 2 + place // 2 if axis == "z" else place


def ring_place(axis):
    if axis == "z":
        return lax.axis_index("z_hi") * 2 + lax.axis_index("z_lo")
    return lax.axis_index(axis)


def shift(value, axis, step, mirrored):
    pairs = []
    for place in range(4):
        for core in range(2):
            target = (place + (-step if mirrored and core else step)) % 4
            pairs.append((along(axis, place) * 2 + core, along(axis, target) * 2 + core))
    return lax.ppermute(value, RING[axis] + ("core",), pairs)


def swap(value, axis):
    return lax.ppermute(value, axis, [(0, 1), (1, 0)])


def put(blocks, block, index):
    return lax.dynamic_update_slice_in_dim(blocks, block[None], index, axis=0)


def take(blocks, index):
    return lax.dynamic_index_in_dim(blocks, index, axis=0, keepdims=False)


def direction():
    return jnp.where(lax.axis_index("core") == 0, 1, 3)


def by_core(mine, other):
    first = lax.axis_index("core") == 0
    return jnp.where(first, mine, other), jnp.where(first, other, mine)


def halves(array):
    rows, columns = array.shape
    return array.reshape(rows, 2, columns // 2).transpose(1, 0, 2)


def chunks(array, width):
    *lead, rows, columns = array.shape
    count = columns // width
    cut = jnp.moveaxis(array.reshape(*lead, rows, count, width), -2, -3)
    return cut.reshape(*lead, count * rows, width)


def pad_rows(array, rows):
    return jnp.pad(array, ((0, rows - array.shape[0]), (0, 0)))


def share(block, axes):
    count = lax.axis_size(axes)
    spread = jnp.broadcast_to(block[None], (count,) + block.shape)
    return lax.all_to_all(spread, axes, 0, 0)


def ring_share(block, axis):
    back = [shift(block, axis, step, False) for step in (3, 2, 1)] + [block]
    return lax.dynamic_slice_in_dim(jnp.stack(back + back[:3]), 3 - ring_place(axis), 4)


def sum_shares(blocks, axes):
    return jnp.sum(lax.all_to_all(blocks, axes, 0, 0).astype(F32), axis=0)


def after(value, *earlier):
    return lax.optimization_barrier((value,) + earlier)[0]


def join_kernel(*refs):
    ins, out = refs[:-1], refs[-1]
    for side in range(2):
        rows = [r[...].astype(F32).reshape(1, -1) for r in ins[side * 9 : side * 9 + 9]]
        rows.append(jnp.zeros((1, 128 - sum(r.shape[1] for r in rows)), F32))
        out[:, side * 128 : side * 128 + 128] = jnp.concatenate(rows, axis=1).astype(BF16)


def join(vectors):
    return pl.pallas_call(join_kernel, out_shape=jax.ShapeDtypeStruct((1, 256), BF16))(*vectors)


def in_hbm(array):
    return pltpu.with_memory_space_constraint(array, pltpu.HBM)


def made_in(shape):
    return pltpu.HBM(shape, BF16) if shape[-2] in (336, 576) else jax.ShapeDtypeStruct(shape, BF16)


def core_id():
    return lax.axis_index("core").astype(jnp.int32).reshape(1)


def direct_sum(blocks, axis):
    me = ring_place(axis)
    total = take(blocks, me).astype(F32)
    for step in (1, 2, 3):
        total = total + shift(take(blocks, (me + step) % 4), axis, step, False).astype(F32)
    return total.astype(BF16)


def together(*values):
    return lax.optimization_barrier(values)


def held_kernel(value, *rest):
    pass


def hold(value, *earlier):
    anywhere = pl.BlockSpec(memory_space=pl.ANY)
    large = pl.BlockSpec(memory_space=pltpu.HBM)
    return pl.pallas_call(
        held_kernel,
        out_shape=jax.ShapeDtypeStruct(value.shape, value.dtype),
        in_specs=[anywhere] + [large if e.shape[-2:] in ((336, 256), (576, 256), (960, 256)) else anywhere for e in earlier],
        out_specs=anywhere,
        input_output_aliases={0: 0},
    )(value, *earlier)


def on_each_core(core_ref, mine, other, work):
    @pl.when(core_ref[0] == 0)
    def _():
        work((mine, other))

    @pl.when(core_ref[0] != 0)
    def _():
        work((other, mine))


def pack_enc_kernel(raw, out):
    def rows_of(first, last, rows):
        return [raw[y, c, :, first:last].astype(F32)[:rows] for y in range(4) for c in range(2)]

    for j in range(13):
        at = j * 48
        out[at : at + 48, :] = jnp.concatenate(rows_of(j * 256, j * 256 + 256, 6), axis=0).astype(BF16)
    parts = []
    for y in range(4):
        for c in range(2):
            for g in range(3):
                parts.append(raw[y, c, :, 3328 + g * 384 : 3712 + g * 384].astype(F32))
    down = jnp.concatenate(parts, axis=0).astype(BF16)
    out[624:816, :] = down[:, :256]
    out[816:912, :128] = down[:96, 256:]
    out[816:912, 128:] = down[96:, 256:]


def pack_enc(raw):
    return pl.pallas_call(
        pack_enc_kernel,
        out_shape=jax.ShapeDtypeStruct((912, 256), BF16),
        compiler_params=pltpu.CompilerParams(vmem_limit_bytes=24 << 20),
    )(raw)


def unpack_call(kernel, part, block, index, outs):
    return pl.pallas_call(
        kernel,
        out_shape=[jax.ShapeDtypeStruct(o, BF16) for o in outs],
        grid_spec=pltpu.PrefetchScalarGridSpec(
            num_scalar_prefetch=1,
            grid=(2, 4),
            in_specs=[pl.BlockSpec(block, index)] * 2,
            out_specs=[pl.BlockSpec((o[0] // 8, o[1]), lambda zl, x, c: (zl * 4 + x, 0)) for o in outs],
        ),
        compiler_params=pltpu.CompilerParams(vmem_limit_bytes=16 << 20),
    )(core_id(), in_hbm(part), swap(part, "core"))


def unpack_enc_kernel(core_ref, mine, other, qkv, out, embed, up, down):
    def work(sides):
        for zh in range(2):
            rows = slice(zh * 48, zh * 48 + 48)
            for j in range(14):
                at = j % 7 * 48
                value = sides[j // 7][0, zh, 0, at : at + 48, :]
                target, k = (qkv, j) if j < 9 else (out, j - 9) if j < 12 else (embed, j - 12)
                target[rows, k * 256 : k * 256 + 256] = value
            for j in range(12):
                at = 336 + j % 6 * 48
                up[rows, j * 256 : j * 256 + 256] = sides[j // 6][0, zh, 0, at : at + 48, :]
            for side in range(2):
                ref, at, k = sides[side], side * 384, zh * 192
                down[k : k + 192, at : at + 256] = ref[0, zh, 0, 624:816, :]
                down[k : k + 96, at + 256 : at + 384] = ref[0, zh, 0, 816:912, :128]
                down[k + 96 : k + 192, at + 256 : at + 384] = ref[0, zh, 0, 816:912, 128:]

    on_each_core(core_ref, mine, other, work)


def unpack_enc(part):
    outs = [(768, 2304), (768, 768), (768, 512), (768, 3072), (3072, 768)]
    return unpack_call(
        unpack_enc_kernel, part, (1, 2, 1, 912, 256), lambda zl, x, c: (x, 0, zl, 0, 0), outs)


def unpack_dec_kernel(place_ref, *refs):
    blocks, (qkv, out, up, down, wide) = (refs[:4], refs[4:8]), refs[8:]
    for which in range(2):
        side = place_ref[0] if which == 0 else 1 - place_ref[0]
        for step in range(4):
            y = lax.rem(place_ref[1] + jnp.where(side == 0, 4 - step, step), 4)
            for zh in range(2):
                ref, k = blocks[which][step], zh * 4 + y
                values = ref[0, zh, 0, 0:64, :].astype(F32)
                for j in range(8):
                    wide[pl.ds(pl.multiple_of(k * 8, 8), 8), j * 256 : j * 256 + 256] = values[j * 8 : j * 8 + 8]
                down[
                    pl.ds(pl.multiple_of(k * 32, 32), 32), pl.ds(pl.multiple_of(side * 256, 256), 256)
                ] = ref[0, zh, 0, 64:96, :]

        def store(number):
            whole = wide[...].astype(BF16)
            if number == 0:
                qkv[:, :1024] = whole[:, :1024]
            else:
                qkv[:, 1024:] = whole[:, :512]
                out[...] = whole[:, 512:1024]
            up[:, number * 1024 : number * 1024 + 1024] = whole[:, 1024:]

        pl.when(side == 0)(functools.partial(store, 0))
        pl.when(side == 1)(functools.partial(store, 1))


def unpack_dec(mine, other):
    outs = [(512, 1536), (512, 512), (512, 2048), (2048, 512)]
    place = jnp.stack([lax.axis_index("core"), ring_place("y")]).astype(jnp.int32)
    return pl.pallas_call(
        unpack_dec_kernel,
        out_shape=[jax.ShapeDtypeStruct(o, BF16) for o in outs],
        grid_spec=pltpu.PrefetchScalarGridSpec(
            num_scalar_prefetch=1,
            grid=(2, 4),
            in_specs=[pl.BlockSpec((1, 2, 1, 96, 256), lambda zl, x, c: (x, 0, zl, 0, 0))] * 8,
            out_specs=[pl.BlockSpec((o[0] // 8, o[1]), lambda zl, x, c: (zl * 4 + x, 0)) for o in outs],
            scratch_shapes=[pltpu.VMEM((64, 2048), F32)],
        ),
        compiler_params=pltpu.CompilerParams(vmem_limit_bytes=16 << 20),
    )(place, *mine, *other)


def cut(array):
    both = halves(array)
    core = lax.axis_index("core")
    return take(both, core), take(both, 1 - core)


def gather_enc(enc6, enc_up, enc_down, vector):
    def enc(which):
        rows = [pad_rows(p, 8) for p in (cut(enc6)[which], cut(enc_up)[which])]
        tall = cut(enc_down)[which].reshape(3, 8, -1).transpose(1, 0, 2).reshape(8, -1)
        return jnp.concatenate(rows + [tall, pad_rows(cut(vector)[which], 8)], axis=1)

    raw = jnp.stack(by_core(enc(0), swap(enc(1), "core")))
    raw = ring_share(raw, "y")
    part = lax.all_gather(pack_enc(raw), ("x", "z_hi", "z_lo"), tiled=False).reshape(4, 2, 2, 912, 256)
    return part, raw[:, :, 0, 4480:].reshape(8, 128)


def gather_patch(patch, stats):
    mine, other = cut(patch)
    rows = jnp.concatenate(by_core(mine, swap(other, "core")), axis=0)
    flat = stats.reshape(1, -1)
    high = lax.reduce_precision(flat, 8, 7)
    mid = lax.reduce_precision(flat - high, 8, 7)
    three = jnp.concatenate([high, mid, flat - high - mid], axis=0)
    three = jnp.pad(three, ((0, 5), (0, rows.shape[1] - three.shape[1]))).astype(BF16)
    blocks = share(jnp.concatenate([rows, three], axis=0), ("x", "z_hi", "y"))
    stats = jnp.sum(blocks[:, 24:27, : flat.shape[1]].astype(F32), axis=(0, 1)).reshape(stats.shape)
    rows = blocks[:, :24].reshape(-1, rows.shape[1])
    return jnp.concatenate(by_core(rows, swap(rows, "core")), axis=1), stats


def gather_dec(dec4, dec_up, dec_down, vectors, started):
    def dec(which):
        wide = jnp.concatenate([cut(dec4)[which], cut(dec_up)[which]], axis=1)
        return wide, cut(dec_down)[which]

    mine, other = dec(0), dec(1)
    wide = jnp.concatenate(by_core(mine[0], swap(other[0], "core")), axis=0)
    tall = jnp.concatenate(by_core(mine[1], swap(other[1], "core")), axis=0)
    vectors = jnp.pad(vectors, ((0, 0), (0, 128)))
    part = after(jnp.concatenate([chunks(wide, 256), tall, vectors], axis=0), started)
    part = share(part, ("x", "z_hi", "z_lo"))
    vectors = part[:, 96:, :128].reshape(128, 128)
    low, high = by_core(vectors, swap(vectors, "core"))
    return part[:, :96].reshape(4, 2, 2, 96, 256), jnp.concatenate([low, high], axis=1)


def spread_kernel(vectors, *outs):
    values = vectors[...]
    for side, unit in ((0, 6), (1, 4)):
        for k, (times, first, count) in enumerate(((1, 0, 7), (2, 7, 1), (4, 9, 1))):
            size = unit * times
            length = size * 128
            place = lax.broadcasted_iota(jnp.int32, (128, length), 1)
            row = lax.broadcasted_iota(jnp.int32, (128, length), 0)
            device = (row & 8) * 8 + (row >> 5) * 16 + (row & 16) // 2 + (row & 7)
            lifted = (place >= device * size) & (place < device * size + size)
            table = lax.dot_general(
                values[:, side * 128 : side * 128 + 128], lifted.astype(BF16),
                (((0,), (0,)), ((), ())), preferred_element_type=F32)
            inside = place[:1] - lax.div(place[:1], size) * size
            for n in range(count):
                wanted = row == inside + (first + n) * unit
                outs[side * 3 + k][n : n + 1, :] = jnp.sum(jnp.where(wanted, table, 0.0), axis=0, keepdims=True)


def spread(vectors):
    shapes = [(8, 768), (1, 1536), (1, 3072), (8, 512), (1, 1024), (1, 2048)]
    return pl.pallas_call(
        spread_kernel,
        out_shape=[jax.ShapeDtypeStruct(s, F32) for s in shapes],
        compiler_params=pltpu.CompilerParams(vmem_limit_bytes=24 << 20),
    )(vectors)


def collect_kernel(*refs):
    ins, out = refs[:-1], refs[-1]
    for side, unit in ((0, 6), (1, 4)):
        total = jnp.zeros((128, 128), F32)
        for k, (times, first, count) in enumerate(((1, 0, 7), (2, 7, 1), (4, 9, 1))):
            size = unit * times
            length = size * 128
            place = lax.broadcasted_iota(jnp.int32, (128, length), 1)
            row = lax.broadcasted_iota(jnp.int32, (128, length), 0)
            lifted = (place >= row * size) & (place < row * size + size)
            inside = place[:1] - lax.div(place[:1], size) * size
            table = jnp.zeros((128, length), F32)
            for n in range(count):
                given = ins[side * 9 + n + (0, 7, 8)[k]][...].reshape(1, -1)
                table = jnp.where(row == inside + (first + n) * unit, given, table)
            total = total + lax.dot_general(
                lifted.astype(BF16), table.astype(BF16), (((1,), (1,)), ((), ())), preferred_element_type=F32)
        out[:, side * 128 : side * 128 + 128] = total.astype(BF16)


def collect(*vectors):
    return pl.pallas_call(
        collect_kernel,
        out_shape=jax.ShapeDtypeStruct((128, 256), BF16),
        compiler_params=pltpu.CompilerParams(vmem_limit_bytes=24 << 20),
    )(*vectors)


def wide_grad_kernel(order, rows, lhs, rhs, *rest):
    out, turned = rest[-2:]

    @pl.when(pl.program_id(0) == 0)
    def _():
        turned[...] = lhs[...].T

    result = jnp.dot(turned[...], rhs[0], preferred_element_type=F32).astype(BF16)
    for block in range(16):
        zl, x, zh = block // 8, block // 2 % 4, block % 2
        spot = (0, x, zh, zl) if order == "xz" else (0, zh, zl, x)
        out[spot] = result[block * rows : block * rows + rows]


def wide_grad(lhs, rhs, buffer, shape, order, rows, row_block, first, per_side):
    length, height = lhs.shape
    parts, _, width = rhs.shape
    per_part = width // 256
    block = (1, 4, 2, 2, rows, 256) if order == "xz" else (1, 2, 2, 4, rows, 256)

    def place(j):
        chunk = j + first
        return (chunk // per_side, 0, 0, 0, row_block + chunk % per_side, 0)

    given = () if buffer is None else (buffer,)
    return pl.pallas_call(
        functools.partial(wide_grad_kernel, order, rows),
        out_shape=made_in(shape),
        grid=(parts * per_part,),
        in_specs=[
            pl.BlockSpec((length, height), lambda j: (0, 0)),
            pl.BlockSpec((1, length, 256), lambda j: (j // per_part, 0, j % per_part)),
        ] + [pl.BlockSpec(memory_space=pltpu.HBM if shape[-2] in (336, 576) else pl.ANY)] * len(given),
        out_specs=pl.BlockSpec(block, place),
        scratch_shapes=[pltpu.VMEM((height, length), BF16)],
        input_output_aliases={2: 0} if given else {},
        compiler_params=pltpu.CompilerParams(vmem_limit_bytes=40 << 20),
        cost_estimate=pl.CostEstimate(
            flops=2 * length * height * width * parts, transcendentals=0,
            bytes_accessed=2 * (length * height + parts * length * width + parts * height * width)),
    )(lhs, rhs, *given)


def tall_grad_kernel(lhs, rhs, out, turned):
    @pl.when(pl.program_id(0) == 0)
    def _():
        turned[...] = lhs[...].T

    result = jnp.dot(turned[...], rhs[...], preferred_element_type=F32).astype(BF16)
    for block in range(16):
        zl, x, zh = block // 8, block // 2 % 4, block % 2
        out[0, x, zh, zl, :, :128] = result[block * 192 : block * 192 + 96]
        out[0, x, zh, zl, :, 128:] = result[block * 192 + 96 : block * 192 + 192]


def tall_grad(lhs, rhs, shape):
    length, height = lhs.shape
    return pl.pallas_call(
        tall_grad_kernel,
        out_shape=made_in(shape),
        grid=(6,),
        in_specs=[pl.BlockSpec((length, height), lambda j: (0, 0)), pl.BlockSpec((length, 128), lambda j: (0, j))],
        out_specs=pl.BlockSpec((1, 4, 2, 2, 96, 256), lambda j: (j // 3, 0, 0, 0, j % 3, 0)),
        scratch_shapes=[pltpu.VMEM((height, length), BF16)],
        compiler_params=pltpu.CompilerParams(vmem_limit_bytes=40 << 20),
        cost_estimate=pl.CostEstimate(
            flops=2 * length * height * rhs.shape[1], transcendentals=0, bytes_accessed=4 * height * rhs.shape[1]),
    )(lhs, rhs)


def add_cores_kernel(info, *refs):
    out = refs[-1]
    at = 0
    for mine, got in zip(refs[0:4:2], refs[1:4:2], strict=True):
        rows = got.shape[1]
        out[0, at : at + rows, :] = (mine[0, 0].astype(F32) + got[0].astype(F32)).astype(BF16)
        at += rows


def add_cores(first, second, *earlier):
    core = lax.axis_index("core")
    operands, specs, rows = [], [], 0
    for part, got in (first, second):
        count = part.shape[-2]
        operands += [in_hbm(part.reshape(2, 16, count, 256)), in_hbm(got.reshape(16, count, 256))]
        specs += [
            pl.BlockSpec((1, 1, count, 256), lambda i, info: (info[0], i, 0, 0)),
            pl.BlockSpec((1, count, 256), lambda i, info: (i, 0, 0))]
        rows += count
    return pl.pallas_call(
        add_cores_kernel,
        out_shape=pltpu.HBM((16, rows, 256), BF16),
        grid_spec=pltpu.PrefetchScalarGridSpec(
            num_scalar_prefetch=1,
            grid=(16,),
            in_specs=specs + [pl.BlockSpec(memory_space=pl.ANY)] * len(earlier),
            out_specs=pl.BlockSpec((1, rows, 256), lambda i, info: (i, 0, 0)),
        ),
        compiler_params=pltpu.CompilerParams(vmem_limit_bytes=24 << 20),
    )(core.astype(jnp.int32).reshape(1), *operands, *earlier)


def core_got(part):
    return part, swap(take(part, 1 - lax.axis_index("core")), "core")


def core_sum(part):
    core = lax.axis_index("core")
    got = swap(take(part, 1 - core), "core")
    return (take(part, core).astype(F32) + got.astype(F32)).astype(BF16)


def finish(mine, other):
    return by_core(mine, swap(other, "core"))


def finish_pair(pair):
    core = lax.axis_index("core")
    return finish(take(pair, core), take(pair, 1 - core))


def join_columns(sides, first, last, rows):
    return jnp.concatenate([side[:rows, first:last] for side in sides], axis=1).astype(F32)


def by_row_kernel(arrived, rest, out):
    last = jnp.zeros((336, 256), F32)
    for block in range(16):
        last = last + arrived[block].astype(F32)
    rest = rest[...].astype(F32)
    out[...] = jnp.zeros_like(out)

    def chunk(value, at, rows):
        for k in range(8):
            out[k // 2, k % 2, 0:rows, at : at + 256] = value[k * rows : (k + 1) * rows].astype(BF16)

    for j in range(7):
        chunk(last[j * 48 : j * 48 + 48], j * 256, 6)
    for j in range(6):
        chunk(rest[672 + j * 48 : 720 + j * 48], 1792 + j * 256, 6)
    for k in range(8):
        y, c = k // 2, k % 2
        for g in range(3):
            for j in range(3):
                n = k % 4 * 24 + g * 8
                value = rest[384 + j * 96 + n : 392 + j * 96 + n, k // 4 * 128 : k // 4 * 128 + 128]
                at = 3328 + g * 384 + j * 128
                out[y, c, :, at : at + 128] = value.astype(BF16)
        for j in range(4):
            n = j * 32 + k * 4
            value = jnp.concatenate([rest[n : n + 4], rest[n + 128 : n + 132]], axis=0)
            out[y, c, :, 4480 + j * 256 : 4736 + j * 256] = value.astype(BF16)
        for g in range(2):
            n = 256 + k * 16 + g * 8
            out[y, c, :, 5504 + g * 256 : 5760 + g * 256] = rest[n : n + 8].astype(BF16)


def by_row(arrived, rest):
    return pl.pallas_call(
        by_row_kernel,
        out_shape=jax.ShapeDtypeStruct((4, 2, 8, 6016), BF16),
        compiler_params=pltpu.CompilerParams(vmem_limit_bytes=40 << 20),
    )(arrived, rest)


def outputs_kernel(low, high, qkv, out, embed, up, down, dqkv, dout, dup, ddown):
    for side, ref in ((0, low), (1, high)):
        value = ref[...].astype(F32)
        if side == 0:
            qkv[:, :1792] = value[:6, :1792]
            dqkv[:, :1024] = value[:4, 4480:5504]
        else:
            qkv[:, 1792:] = value[:6, :512]
            out[...] = value[:6, 512:1280]
            embed[...] = value[:6, 1280:1792]
            dqkv[:, 1024:] = value[:4, 4480:4992]
            dout[...] = value[:4, 4992:5504]
        up[:, side * 1536 : side * 1536 + 1536] = value[:6, 1792:3328]
        for g in range(3):
            down[g * 8 : g * 8 + 8, side * 384 : side * 384 + 384] = value[:, 3328 + g * 384 : 3712 + g * 384]
        dup[:, side * 1024 : side * 1024 + 1024] = value[4:, 4480:5504]
        for g in range(2):
            ddown[g * 8 : g * 8 + 8, side * 256 : side * 256 + 256] = value[:, 5504 + g * 256 : 5760 + g * 256]


def outputs(low, high):
    shapes = [(6, 2304), (6, 768), (6, 512), (6, 3072), (24, 768), (4, 1536), (4, 512), (4, 2048), (16, 512)]
    return pl.pallas_call(
        outputs_kernel,
        out_shape=[jax.ShapeDtypeStruct(s, F32) for s in shapes],
        compiler_params=pltpu.CompilerParams(vmem_limit_bytes=24 << 20),
    )(low, high)


def sum_over_y(blocks):
    core = lax.axis_index("core")
    pair = sum_shares(blocks, "y").astype(BF16)
    return outputs(*finish(take(pair, core), take(pair, 1 - core)))


def sum_patch(rows, vectors, earlier):
    pipe = lax.axis_index("z_lo")
    got = swap(take(vectors, 1 - pipe), "z_lo")
    vectors = (take(vectors, pipe).astype(F32) + got.astype(F32)).astype(BF16)
    vectors = vectors.transpose(4, 2, 1, 0, 3, 5)[..., None, :]
    vectors = jnp.pad(vectors, ((0, 0),) * 5 + ((0, 3), (0, 256)))
    rows = rows.astype(BF16).reshape(4, 2, 4, 2, 12, 2, 384).transpose(5, 2, 1, 0, 3, 4, 6)
    part = core_sum(jnp.concatenate([rows, vectors], axis=5))
    part = direct_sum(part, "y")
    zh = lax.axis_index("z_hi")
    got = swap(take(part, 1 - zh), "z_hi")
    part = (take(part, zh).astype(F32) + got.astype(F32)).astype(BF16)
    low, high = finish_pair(direct_sum(hold(part, earlier), "x"))
    return join_columns((low, high), 0, 384, 12), low[12, :128].astype(F32), high[12, :128].astype(F32)


def layer_norm(residual, gain, shift_row):
    center = residual - jnp.mean(residual, axis=-1, keepdims=True)
    spread = jnp.mean(center * center, axis=-1, keepdims=True)
    return center * lax.rsqrt(spread + norm_epsilon) * gain + shift_row


def frequencies(model_width):
    half_width = model_width // 2
    return jnp.exp(jnp.arange(half_width).astype(F32) * (-math.log(10000.0) / half_width))


def position_rows(places, model_width):
    phase_angle = places.astype(F32)[:, None] * frequencies(model_width)[None, :]
    return jnp.concatenate([jnp.sin(phase_angle), jnp.cos(phase_angle)], axis=1)


def dot(left, right):
    return jnp.dot(left, right, preferred_element_type=F32)


def dot_t(left, right):
    return lax.dot_general(left, right, (((1,), (1,)), ((), ())), preferred_element_type=F32)


def t_dot(left, right):
    return lax.dot_general(left, right, (((0,), (0,)), ((), ())), preferred_element_type=F32)


def attend_kernel(size, count_ref, q_ref, k_ref, v_ref, o_ref):
    length = q_ref.shape[0]
    q, k, v = q_ref[...], k_ref[...], v_ref[...]
    kept = lax.broadcasted_iota(jnp.int32, (1, length), 1) < count_ref[0]
    lane = lax.broadcasted_iota(jnp.int32, (1, 128), 1)
    total = jnp.zeros((length, 128), F32)
    for head in range(128 // size):
        mine = (lane >= head * size) & (lane < (head + 1) * size)
        scores = jnp.where(kept, dot_t(jnp.where(mine, q, jnp.zeros_like(q)), k), masked_score)
        weight = jnp.exp2((scores - jnp.max(scores, axis=1, keepdims=True)) * (size ** (-0.5) * LOG2E))
        prob = (weight * (1.0 / jnp.sum(weight, axis=1, keepdims=True))).astype(BF16)
        total = total + dot(prob, jnp.where(mine, v, jnp.zeros_like(v)))
    o_ref[...] = total.astype(BF16)

def attend(qkv, heads, count):
    length, width = qkv.shape[0], qkv.shape[1] // 3
    groups = width // 128
    spec = lambda part: pl.BlockSpec((length, 128), lambda g, c, part=part: (0, part * groups + g))
    return pl.pallas_call(
        functools.partial(attend_kernel, width // heads),
        out_shape=jax.ShapeDtypeStruct((length, width), BF16),
        grid_spec=pltpu.PrefetchScalarGridSpec(
            num_scalar_prefetch=1, grid=(groups,),
            in_specs=[spec(0), spec(1), spec(2)],
            out_specs=pl.BlockSpec((length, 128), lambda g, c: (0, g))),
        compiler_params=pltpu.CompilerParams(vmem_limit_bytes=48 << 20),
    )(count, qkv, qkv, qkv)

def attend_back_kernel(size, count_ref, q_ref, k_ref, v_ref, g_ref, o_ref, turned):
    length = q_ref.shape[0]
    q, k, v, g = q_ref[...], k_ref[...], v_ref[...], g_ref[...]
    k_turned = k.T
    kept = lax.broadcasted_iota(jnp.int32, (length, 1), 0) < count_ref[0]
    lane = lax.broadcasted_iota(jnp.int32, (1, 128), 1)
    dk = jnp.zeros((length, 128), F32)
    dv = jnp.zeros((length, 128), F32)
    zero = jnp.zeros_like(q)
    for head in range(128 // size):
        mine = (lane >= head * size) & (lane < (head + 1) * size)
        q_h, g_h = jnp.where(mine, q, zero), jnp.where(mine, g, zero)
        scores = jnp.where(kept, dot_t(k, q_h), masked_score)
        weight = jnp.exp2((scores - jnp.max(scores, axis=0, keepdims=True)) * (size ** (-0.5) * LOG2E))
        prob = weight * (1.0 / jnp.sum(weight, axis=0, keepdims=True))
        dv = dv + dot(prob.astype(BF16), g_h)
        prob_grad = dot_t(v, g_h)
        inner = jnp.sum(prob * prob_grad, axis=0, keepdims=True)
        score_grad = (prob * (prob_grad - inner)).astype(BF16)
        dk = dk + dot(score_grad, q_h)
        turned[head * size : (head + 1) * size, :] = dot(k_turned[head * size : (head + 1) * size], score_grad)
    o_ref[0] = (turned[...] * size ** (-0.5)).T.astype(BF16)
    o_ref[1] = (dk * size ** (-0.5)).astype(BF16)
    o_ref[2] = dv.astype(BF16)

def attend_back(qkv, grad, heads, count):
    length, width = qkv.shape[0], qkv.shape[1] // 3
    groups = width // 128
    spec = lambda part: pl.BlockSpec((length, 128), lambda g, c, part=part: (0, part * groups + g))
    return pl.pallas_call(
        functools.partial(attend_back_kernel, width // heads),
        out_shape=jax.ShapeDtypeStruct((3, length, width), BF16),
        grid_spec=pltpu.PrefetchScalarGridSpec(
            num_scalar_prefetch=1, grid=(groups,),
            in_specs=[spec(0), spec(1), spec(2), spec(0)],
            out_specs=pl.BlockSpec((3, length, 128), lambda g, c: (0, 0, g)),
            scratch_shapes=[pltpu.VMEM((128, length), F32)]),
        compiler_params=pltpu.CompilerParams(vmem_limit_bytes=56 << 20),
    )(count, qkv, qkv, qkv, grad)


def block_forward(residual, weights, head_count, key_keep):
    (gain1, shift1, qkv_weight, qv_bias, out_weight, out_bias, gain2, shift2, up_weight, up_bias,
     down_weight, down_bias) = weights
    width = residual.shape[1]
    normed = layer_norm(residual, gain1, shift1).astype(BF16)
    qkv_bias = jnp.concatenate([qv_bias[:width], jnp.zeros((width,), F32), qv_bias[width:]])
    qkv_rows = (dot(normed, qkv_weight) + qkv_bias).astype(BF16)
    attended = attend(qkv_rows, head_count, key_keep)
    hidden = residual + (dot(attended, out_weight) + out_bias)
    second = layer_norm(hidden, gain2, shift2).astype(BF16)
    up_proj = dot(second, up_weight) + up_bias
    active = jax.nn.gelu(up_proj).astype(BF16)
    stored = (residual, normed, qkv_rows, attended, hidden, second, up_proj, active)
    return hidden, active, stored


def block_backward(grad_out, stored, weights, head_count, key_keep, send):
    (gain1, shift1, qkv_weight, qv_bias, out_weight, out_bias, gain2, shift2, up_weight, up_bias,
     down_weight, down_bias) = weights
    (residual, normed, qkv_rows, attended, hidden, second, up_proj, active) = stored
    width = residual.shape[1]
    down_branch = grad_out.astype(BF16)
    down_bias_grad = jnp.sum(down_branch.astype(F32), axis=0)
    down_branch = send("down", active, down_branch)
    active_grad = dot_t(down_branch, down_weight)
    up_grad = send("gelu", None, jax.vjp(jax.nn.gelu, up_proj)[1](active_grad)[0].astype(BF16))
    up_bias_grad = jnp.sum(up_grad.astype(F32), axis=0)
    up_grad = send("up", second, up_grad)
    second_grad = dot_t(up_grad, up_weight)
    hidden_grad, gain2_grad, shift2_grad = jax.vjp(layer_norm, hidden, gain2, shift2)[1](second_grad)
    hidden_grad = hidden_grad + grad_out
    attn_branch = hidden_grad.astype(BF16)
    out_bias_grad = jnp.sum(attn_branch.astype(F32), axis=0)
    attn_branch = send("out", attended, attn_branch)
    attended_grad = send("attended", None, dot_t(attn_branch, out_weight).astype(BF16))
    qkv_parts = attend_back(qkv_rows, attended_grad, head_count, key_keep)
    qkv_parts = send("qkv", normed, qkv_parts)
    qkv_grad = jnp.concatenate([qkv_parts[0], qkv_parts[1], qkv_parts[2]], axis=1)
    qkv_sums = jnp.sum(qkv_grad.astype(F32), axis=0)
    qv_bias_grad = jnp.concatenate([qkv_sums[:width], qkv_sums[2 * width :]])
    normed_grad = dot_t(qkv_grad, qkv_weight)
    residual_grad, gain1_grad, shift1_grad = jax.vjp(layer_norm, residual, gain1, shift1)[1](normed_grad)
    residual_grad = residual_grad + hidden_grad
    vectors = (gain1_grad, shift1_grad, out_bias_grad, gain2_grad, shift2_grad, down_bias_grad)
    return residual_grad, vectors, qv_bias_grad, up_bias_grad


def band_sums(pixels, bands):
    items, patches, width = pixels.shape
    view = pixels.reshape(items, patches, bands, width // bands)
    sums = jnp.stack([jnp.sum(view, axis=(0, 1, 3)), jnp.sum(view * view, axis=(0, 1, 3))])
    return sums + swap(sums, "core")


def pixel_kernel(onehot, grad, scale, out):
    placed = lax.dot_general(
        onehot[0], grad[0], (((0,), (0,)), ((), ())), preferred_element_type=F32)
    out[0] = placed[: out.shape[1]] * scale[...]


def place_pixels(onehot, grad, scale, patches):
    items, slots, grid = onehot.shape
    width = grad.shape[2]
    return pl.pallas_call(
        pixel_kernel,
        out_shape=jax.ShapeDtypeStruct((items, patches, width), F32),
        grid=(items,),
        in_specs=[
            pl.BlockSpec((1, slots, grid), lambda i: (i, 0, 0)),
            pl.BlockSpec((1, slots, width), lambda i: (i, 0, 0)),
            pl.BlockSpec((1, width), lambda i: (0, 0)),
        ],
        out_specs=pl.BlockSpec((1, patches, width), lambda i: (i, 0, 0)),
        compiler_params=pltpu.CompilerParams(vmem_limit_bytes=24 << 20),
    )(onehot, grad, scale)


def per_device(
    pixels, visible_counts, visible_index, running_mean, running_var, patch_weight, patch_bias,
    enc_ln1_gain, enc_ln1_shift, enc_qkv_weight, enc_qv_bias, enc_out_weight, enc_out_bias,
    enc_ln2_gain, enc_ln2_shift, enc_up_weight, enc_up_bias, enc_down_weight, enc_down_bias,
    dec_embed_weight, dec_embed_bias, mask_token, dec_ln1_gain, dec_ln1_shift, dec_qkv_weight,
    dec_qv_bias, dec_out_weight, dec_out_bias, dec_ln2_gain, dec_ln2_shift, dec_up_weight,
    dec_up_bias, dec_down_weight, cotangent,
):
    pipe = lax.axis_index("z_lo")
    items, patches, half_pix = pixels.shape
    bands_here = running_mean.shape[0]
    band_pix = half_pix // bands_here
    width, dec_width = patch_weight.shape[1], dec_embed_weight.shape[1]

    vector = join((
        patch_bias, enc_ln1_gain, enc_ln1_shift, enc_out_bias, enc_ln2_gain, enc_ln2_shift, enc_down_bias,
        enc_qv_bias, enc_up_bias, dec_embed_bias, mask_token, dec_ln1_gain, dec_ln1_shift, dec_out_bias,
        dec_ln2_gain, dec_ln2_shift, dec_qv_bias, dec_up_bias))
    enc_part, vector = gather_enc(
        jnp.concatenate([enc_qkv_weight, enc_out_weight, dec_embed_weight], axis=1), enc_up_weight,
        enc_down_weight, vector)
    patch_rows, stats = gather_patch(patch_weight, after(band_sums(pixels, bands_here), vector))
    dec_part, vectors = gather_dec(
        jnp.concatenate([dec_qkv_weight, dec_out_weight], axis=1), dec_up_weight, dec_down_weight, vector,
        stats)
    enc_s, enc_qv, enc_upb, dec_s, dec_qv, dec_upb = spread(vectors)
    enc_qv, enc_upb, dec_qv, dec_upb = enc_qv[0], enc_upb[0], dec_qv[0], dec_upb[0]
    band_view = pixels.reshape(items, patches, bands_here, band_pix)
    band_total, band_square = stats
    population = 64 * items * patches * band_pix
    band_mean = band_total / population
    band_var = band_square / population - band_mean * band_mean
    band_scale = lax.rsqrt(band_var + band_epsilon)
    band_means = 0.9 * running_mean + 0.1 * band_mean
    band_variances = 0.9 * running_var + 0.1 * band_var
    normalized = ((band_view - band_mean[:, None]) * band_scale[:, None]).reshape(items, patches, half_pix)

    index = jnp.pad(visible_index, ((0, 0), (0, SLOTS - visible_index.shape[1])))
    keep = jnp.arange(SLOTS)[None, :] < visible_counts[:, None]
    onehot = (
        (index[:, :, None] == jnp.arange(GRID)[None, None, :]) & keep[:, :, None]
    ).astype(BF16)
    picked = jnp.einsum("ivp,iph->ivh", onehot[:, :, :patches], normalized.astype(BF16),
                        preferred_element_type=F32).astype(BF16)
    embedded = jnp.einsum("ivh,hd->ivd", picked, patch_rows, preferred_element_type=F32).astype(BF16)
    embedded, dec_part = together(embedded, dec_part)
    other_half = swap(take(embedded, 1 - pipe), "z_lo")
    start_rows = (
        take(embedded, pipe).astype(F32) + other_half.astype(F32) + enc_s[0] + position_rows(take(index, pipe), width)
    )
    dec_pos = position_rows(jnp.arange(GRID), dec_width)
    ring = [dec_part, shift(dec_part, "y", 1, True)]
    enc_part, start_rows, ring[1], dec_pos = together(enc_part, start_rows, ring[1], dec_pos)
    ring.append(shift(ring[1], "y", 1, True))
    enc_weights = list(unpack_enc(enc_part))
    enc_qkv, enc_out, embed, enc_up, enc_down = enc_weights
    ring.append(shift(ring[2], "y", 1, True))
    other = [swap(block, "core") for block in ring[:2]]
    encoder = (enc_s[1], enc_s[2], enc_qkv, enc_qv, enc_out, enc_s[3], enc_s[4], enc_s[5], enc_up, enc_upb,
               enc_down, enc_s[6])
    my_onehot = take(onehot, pipe)
    my_count = lax.dynamic_slice_in_dim(visible_counts, pipe, 1)
    start_rows = (
        take(embedded, pipe).astype(F32) + other_half.astype(F32) + enc_s[0] + position_rows(take(index, pipe), width)
    )
    hidden, active, enc_stored = block_forward(start_rows, encoder, HEADS, my_count)
    ring[2:] = [hold(block, hidden) for block in ring[2:]]
    other += [swap(block, "core") for block in ring[2:]]
    dec_qkv, dec_out, dec_up, dec_down = unpack_dec(ring, other)
    decoder = (dec_s[2], dec_s[3], dec_qkv, dec_qv, dec_out, dec_s[4], dec_s[5], dec_s[6], dec_up, dec_upb,
               dec_down, jnp.zeros((dec_width,), F32))
    encoded = (hidden + (dot(active, enc_down) + encoder[11])).astype(BF16)
    latent = (dot(encoded, embed) + dec_s[0]).astype(BF16)
    covered = jnp.sum(my_onehot.astype(F32), axis=0)
    bare = jnp.where(jnp.arange(GRID) < patches, 1.0 - covered, 0.0)[:, None]
    grid = t_dot(my_onehot, latent) + bare * dec_s[1] + dec_pos
    grid_count = jnp.full((1,), patches, jnp.int32)
    _, _, dec_stored = block_forward(grid, decoder, DHEADS, grid_count)
    target = jnp.pad(take(cotangent, pipe), ((0, GRID - patches), (0, 0)))
    shape_d, shape_a, shape_b = (2, 4, 2, 2, 384, 256), (2, 4, 2, 2, 336, 256), (2, 4, 2, 2, 576, 256)
    sent = {}

    def send_dec(name, lhs, rhs):
        if name in ("gelu", "attended"):
            return rhs
        if name == "qkv":
            sent["d"] = wide_grad(lhs, rhs, sent["d"], shape_d, "xz", 32, 0, 0, 4)
            return rhs
        place = {"down": (128, 2, 0, 1), "up": (32, 4, 0, 4), "out": (32, 0, 6, 4)}[name]
        sent["d"] = wide_grad(lhs, rhs[None], sent.get("d"), shape_d, "xz", *place)
        return rhs

    grid_grad, (dg1, ds1, dob, dg2, ds2, _), dqv, dub = block_backward(
        target, dec_stored, decoder, DHEADS, grid_count, send_dec)
    mask_grad = jnp.sum(bare * grid_grad, axis=0)
    latent_grad = dot(my_onehot, grid_grad.astype(BF16)).astype(BF16)
    embed_bias_grad = jnp.sum(latent_grad.astype(F32), axis=0)
    encoded_grad = dot_t(latent_grad, embed).astype(BF16).astype(F32)
    encoded_grad = hold(encoded_grad, sent["d"])
    part_d = core_got(sent["d"])

    def send_enc(name, lhs, rhs):
        if name == "down":
            sent["feed"] = tall_grad(lhs, rhs, shape_b)
        if name == "up":
            sent["feed"] = wide_grad(lhs, rhs[None], sent["feed"], shape_b, "xz", 48, 6, 0, 6)
            rhs = hold(rhs, sent["feed"])
            sent["feed"] = core_got(sent["feed"])
        if name == "out":
            part = wide_grad(encoded, latent_grad[None], None, shape_a, "xz", 48, 0, 12, 7)
            sent["a"] = wide_grad(lhs, rhs[None], part, shape_a, "xz", 48, 0, 9, 7)
        if name == "attended":
            rest = add_cores(part_d, sent["feed"], rhs)
            rhs = hold(rhs, rest)
            sent["rest"] = lax.psum_scatter(rest.reshape(-1, 256), ("x", "z_hi", "z_lo"), tiled=True)
        if name == "qkv":
            part = wide_grad(lhs, rhs, sent["a"], shape_a, "xz", 48, 0, 0, 7)
            rhs = hold(rhs, part)
            sent["a"] = core_sum(part)
        return rhs

    start_grad, (eg1, es1, eob, eg2, es2, edb), eqv, eub = block_backward(
        encoded_grad, enc_stored, encoder, HEADS, my_count, send_enc)
    start_low = hold(start_grad.astype(BF16), sent["a"])
    start_other = swap(start_low, "z_lo")
    arrived = lax.all_to_all(sent["a"].reshape(16, 336, 256), ("x", "z_hi", "z_lo"), 0, 0)
    blocks = by_row(arrived, sent["rest"])
    patch_bias_grad = jnp.sum(start_low.astype(F32), axis=0)
    start_pair = jnp.where(pipe == 0, jnp.stack([start_low, start_other]), jnp.stack([start_other, start_low]))
    vector_grads = collect(
        patch_bias_grad, eg1, es1, eob, eg2, es2, edb, eqv, eub,
        embed_bias_grad, mask_grad, dg1, ds1, dob, dg2, ds2, dqv, dub)
    out_patch, ev, dv = sum_patch(
        t_dot(picked.reshape(-1, half_pix), start_pair.reshape(-1, width)),
        vector_grads.reshape(2, 4, 2, 4, 2, 2, 128), blocks)
    start_pair = hold(start_pair, blocks)
    picked_grad = jnp.einsum("ivd,hd->ivh", start_pair, patch_rows, preferred_element_type=F32).astype(BF16)
    pixel_grad = place_pixels(onehot, picked_grad, jnp.repeat(band_scale, band_pix)[None], patches)
    (out_qkv, out_out, out_embed, out_up, out_down, out_dqkv, out_dout, out_dup, out_ddown) = sum_over_y(blocks)
    return (
        band_means, band_variances, pixel_grad, out_patch, ev[:6], ev[6:12], ev[12:18],
        out_qkv, ev[42:54], out_out, ev[18:24], ev[24:30], ev[30:36],
        out_up, ev[54:78], out_down, ev[36:42], out_embed, dv[:4], dv[4:8], dv[8:12], dv[12:16],
        out_dqkv, dv[28:36], out_dout, dv[16:20], dv[20:24], dv[24:28],
        out_dup, dv[36:52], out_ddown,
    )


def solution(mesh):
    whole = P(ALL)
    sizes = (2, 4, 2, 4, 2)
    cube = Mesh(mesh.devices.reshape(sizes), ALL)
    placed = (P(DP, None, "z_lo"), P(DP), P(DP, None), P("z_lo"), P("z_lo")) + (whole,) * 28 + (P(DP, None, None),)
    return jax.shard_map(
        per_device,
        mesh=cube,
        in_specs=placed,
        out_specs=(P("z_lo"), P("z_lo"), P(DP, None, "z_lo")) + (whole,) * 28,
        check_vma=False,
    )
```
